512 devices in a mesh: dp: 16 (over z_lo, core), row: 4 (over y), col: 8 (over z_hi, x).
Axes of the slice: x: 4, y: 4, z: 16 (z_hi: 2, z_lo: 8; z = z_hi * 8 + z_lo), core: 2. Of those that a mesh axis runs over, the one named last changes fastest.
Arguments:
- tokens: bfloat16 [12288, 16384], P('dp', 'col'), may hold values from -6 to 6
- out_grad: bfloat16 [12288, 16384], P('dp', 'col'), may hold values from -6 to 6
- router_logits: float32 [98304], P('dp'), may hold values from -8 to 8
- routed_counts: int32 [16], P('dp'), may hold values from 192 to 768, as said below
- routed_positions: int32 [12288], P('dp'), may hold values from 0 to 6143, as said below
- gate_values: bfloat16 [16384, 512], P(('col', 'dp'), 'row'), may hold values from -4 to 4
- up_values: bfloat16 [16384, 512], P(('col', 'dp'), 'row'), may hold values from -4 to 4
- down_values: bfloat16 [512, 16384], P('row', ('col', 'dp')), may hold values from -4 to 4
- gate_scales: float32 [128, 4], P('col', 'row'), may hold values from 0.00390625 to 0.015625
- up_scales: float32 [128, 4], P('col', 'row'), may hold values from 0.00390625 to 0.015625
- down_scales: float32 [4, 128], P('row', 'col'), may hold values from 0.00390625 to 0.015625
Outputs:
- grad_tokens: bfloat16 [12288, 16384], P('dp', 'col')
- grad_gate: float32 [16384, 512], P(('col', 'dp'), 'row')
- grad_up: float32 [16384, 512], P(('col', 'dp'), 'row')
- grad_down: float32 [512, 16384], P('row', ('col', 'dp'))
- grad_logits: float32 [98304], P('dp')
The draws below stay inside these ranges and needn't reach their ends.
Inputs may be any that keep to these rules, and one draw needn't show every extreme that they name: `routed_counts`: live routed rows of each data group; in every draw some group has all 768 rows live. `routed_positions`: within each data group, 768 distinct positions in increasing order, 0 and 6143 among them; slots at or past the group's count are padding.
All inputs are finite; a program needn't handle non-finite values.
Results may differ from the reference program's by a relative error of at most 0.0075.
Values may be sent and summed in bfloat16 or wider, within the bound.
No kernel may reach another device: no remote copies, remote signals or barrier semaphores. Data moves between devices by JAX's collectives and lax.ppermute only.
A program may use at most 128 MiB of HBM per device.

```python
import math
import jax
import jax.numpy as jnp
from jax import lax

D = 16384
QB = 128
CAP = 768
F = 512
SEQ = 6144
N_DP = 16


def draw_routed_counts(key, part):
    key = jax.random.fold_in(key, 11)
    key_counts, key_full = jax.random.split(key)
    counts = jax.random.randint(key_counts, (N_DP,), CAP // 4, CAP + 1)
    full_group = jax.random.randint(key_full, (), 0, N_DP)
    return jnp.where(jnp.arange(N_DP) == full_group, CAP, counts).astype(jnp.int32)


def draw_routed_positions(key, part):
    key = jax.random.fold_in(key, 23)
    group_keys = jax.random.split(key, N_DP)

    def per_group(group_key):
        middle_positions = jax.random.permutation(group_key, SEQ - 2)[:CAP - 2].astype(jnp.int32) + 1
        chosen = jnp.concatenate([jnp.zeros((1,), jnp.int32), middle_positions, jnp.full((1,), SEQ - 1, jnp.int32)])
        return jnp.sort(chosen)
    return jax.vmap(per_group)(group_keys).reshape(N_DP * CAP).astype(jnp.int32)


def with_spikes(drawn, own_key, source, target, shards_of, factor):
    owner, partner = [(jnp.arange(drawn.shape[position]) // (drawn.shape[position] // shards_of)).reshape([-1 if axis == position else 1 for axis in range(drawn.ndim)]) for position in (source, target)]
    chosen = jax.random.permutation(own_key, shards_of)[partner]
    strong = (owner == chosen) | (owner == (partner + shards_of // 2) % shards_of)
    return jnp.where(strong, factor * drawn, drawn)


def block_scale(own_key, extent, cuts, low, largest):
    def one(dim, shards_of):
        heights = jax.random.uniform(jax.random.fold_in(jax.random.fold_in(own_key, 6), dim), (shards_of,), jnp.float32, low / len(cuts), largest / len(cuts))
        return jnp.repeat(jnp.exp(heights), extent[dim] // shards_of).reshape((-1,) + (1,) * (len(extent) - dim - 1))

    factor_of = one(*cuts[0])
    for cut in cuts[1:]:
        factor_of = factor_of * one(*cut)
    return factor_of


def centred(stream_key, shape, scale, bound, cuts=(), dtype=jnp.bfloat16):
    loudness = block_scale(stream_key, shape, cuts, -0.22, 0.18) if cuts else 1.0
    result = jax.random.normal(stream_key, shape, jnp.float32) * scale * loudness
    return jnp.minimum(jnp.maximum(result, -bound), bound).astype(dtype)


def heavy_noise(stream_key, extent, spread, reach, shards, heavy, held_as=jnp.bfloat16):
    entries = spread * jax.random.normal(stream_key, extent, jnp.float32)
    if shards:
        entries = entries * block_scale(stream_key, extent, shards, -0.22, 0.18)
    return jnp.clip(with_spikes(entries, jax.random.fold_in(stream_key, 3), *heavy), -reach, reach).astype(held_as)


def setup_inputs(seed: int = 0) -> dict:
    arg_keys = jax.random.split(jax.random.key(seed), 12)
    return {
        "tokens": heavy_noise(arg_keys[0], (N_DP * CAP, D), 1.0, 6.0, ((0, 16), (1, 8)), (0, 1, 16, 2.0)),
        "out_grad": centred(arg_keys[1], (N_DP * CAP, D), 1.0, 6.0, ((0, 16), (1, 8))),
        "router_logits": centred(arg_keys[2], (N_DP * SEQ,), 2.0, 8.0, ((0, 16),), jnp.float32),
        "routed_counts": draw_routed_counts(jax.random.fold_in(arg_keys[11], 71), 0),
        "routed_positions": draw_routed_positions(jax.random.fold_in(arg_keys[11], 71), 0),
        "gate_values": centred(arg_keys[5], (D, F), 1.0, 4.0, ((0, 128), (1, 4))),
        "up_values": centred(arg_keys[6], (D, F), 1.0, 4.0, ((0, 128), (1, 4))),
        "down_values": centred(arg_keys[7], (F, D), 1.0, 4.0, ((0, 4), (1, 128))),
        "gate_scales": jnp.clip(jnp.exp(math.log(0.015625) - 1.3862944 * jax.random.uniform(arg_keys[8], (D // QB, F // QB), jnp.float32) ** block_scale(arg_keys[8], (D // QB, F // QB), ((0, 8), (1, 4)), -0.2, 0.2)), 0.00390625, 0.015625),
        "up_scales": jnp.clip(jnp.exp(math.log(0.015625) - 1.3862944 * jax.random.uniform(arg_keys[9], (D // QB, F // QB), jnp.float32) ** block_scale(arg_keys[9], (D // QB, F // QB), ((0, 8), (1, 4)), -0.2, 0.2)), 0.00390625, 0.015625),
        "down_scales": jnp.clip(jnp.exp(math.log(0.015625) - 1.3862944 * jax.random.uniform(arg_keys[10], (F // QB, D // QB), jnp.float32) ** block_scale(arg_keys[10], (F // QB, D // QB), ((0, 4), (1, 8)), -0.2, 0.2)), 0.00390625, 0.015625),
    }


def dequantize(values, scales):
    height, breadth = values.shape
    row_blocks, col_blocks = scales.shape
    quant_tiles = values.astype(jnp.float32).reshape(row_blocks, height // row_blocks, col_blocks, breadth // col_blocks)
    return (quant_tiles * scales[:, None, :, None]).reshape(height, breadth).astype(jnp.bfloat16)


def reference(tokens, out_grad, router_logits, routed_counts, routed_positions, gate_values, up_values, down_values, gate_scales, up_scales, down_scales):
    w_gate = dequantize(gate_values, gate_scales)
    w_up = dequantize(up_values, up_scales)
    w_down = dequantize(down_values, down_scales)
    model_width = tokens.shape[1]
    inner_width = gate_values.shape[1]

    def one_group(totals, inputs):
        token_rows, grad_rows, logits, row_count, positions = inputs
        live_rows = (jnp.arange(CAP) < row_count).astype(jnp.float32)
        router_rate = jax.nn.sigmoid(logits[positions])
        row_weight = router_rate * live_rows
        gate_sum = jnp.dot(token_rows, w_gate, preferred_element_type=jnp.float32)
        up_sum = jnp.dot(token_rows, w_up, preferred_element_type=jnp.float32)
        back_sum = jnp.dot(grad_rows, w_down.T, preferred_element_type=jnp.float32)
        gate_sigmoid = jax.nn.sigmoid(gate_sum)
        activated = gate_sum * gate_sigmoid
        hidden_full = activated * up_sum
        hidden = hidden_full.astype(jnp.bfloat16)
        hidden_delta = back_sum * row_weight[:, None]
        up_delta = (hidden_delta * activated).astype(jnp.bfloat16)
        gate_delta = (hidden_delta * up_sum * gate_sigmoid * (1.0 + gate_sum * (1.0 - gate_sigmoid))).astype(jnp.bfloat16)
        scaled_grad = (grad_rows.astype(jnp.float32) * row_weight[:, None]).astype(jnp.bfloat16)
        grad_tokens = (jnp.dot(gate_delta, w_gate.T, preferred_element_type=jnp.float32)
                       + jnp.dot(up_delta, w_up.T, preferred_element_type=jnp.float32)).astype(jnp.bfloat16)
        router_delta = jnp.sum(back_sum * hidden_full, axis=1)
        logit_delta = router_delta * router_rate * (1.0 - router_rate) * live_rows
        grad_logits = jnp.zeros((SEQ,), jnp.float32).at[positions].add(logit_delta)
        gate_term = lax.optimization_barrier(jnp.dot(token_rows.T, gate_delta, preferred_element_type=jnp.float32).astype(jnp.bfloat16))
        up_term = lax.optimization_barrier(jnp.dot(token_rows.T, up_delta, preferred_element_type=jnp.float32).astype(jnp.bfloat16))
        down_term = lax.optimization_barrier(jnp.dot(hidden.T, scaled_grad, preferred_element_type=jnp.float32).astype(jnp.bfloat16))
        new_totals = (totals[0] + gate_term.astype(jnp.float32),
                      totals[1] + up_term.astype(jnp.float32),
                      totals[2] + down_term.astype(jnp.float32))
        return new_totals, (grad_tokens, grad_logits)

    start_totals = (jnp.zeros((model_width, inner_width), jnp.float32),
                    jnp.zeros((model_width, inner_width), jnp.float32),
                    jnp.zeros((inner_width, model_width), jnp.float32))
    totals, outputs = lax.scan(one_group, start_totals,
                               (tokens.reshape(N_DP, CAP, model_width),
                                out_grad.reshape(N_DP, CAP, model_width),
                                router_logits.reshape(N_DP, SEQ),
                                routed_counts,
                                routed_positions.reshape(N_DP, CAP)))
    grad_tokens, grad_logits = outputs
    return (grad_tokens.reshape(N_DP * CAP, model_width), totals[0], totals[1], totals[2],
            grad_logits.reshape(N_DP * SEQ))
```

```python
import jax
import jax.numpy as jnp
from jax import lax
from jax.experimental import pallas as pl
from jax.experimental.pallas import tpu as pltpu
from jax.sharding import Mesh, PartitionSpec as P

BF = jnp.bfloat16
F32 = jnp.float32
Z, CORES, ROWS, Z_HI, XS = 8, 2, 4, 2, 4
T = 128
CAP = 768
D = 2048
RB = CAP // XS
MSG = RB + 16
AXES = ("z", "core", "row", "zhi", "x")
NT = (((1,), (1,)), ((), ()))
VMEM_LIMIT = 44 * 1024 * 1024


def swap(value, axis, size, mask):
    return lax.ppermute(value, axis, [(i, i ^ mask) for i in range(size)])


def far_first(i):
    return ((i & 1) << 2) | (i & 2) | ((i >> 2) & 1)


def tile_kernel(ids, gs, us, ds, gate, up, down, out):
    dp = ids[0] * CORES + ids[1]
    out[:, 0:T] = (gate[...].astype(F32) * gs[dp, 0]).astype(BF)
    out[:, T : 2 * T] = (up[...].astype(F32) * us[dp, 0]).astype(BF)
    out[:, 2 * T : 3 * T] = (down[...].astype(F32) * ds[0, dp]).T.astype(BF)


def own_tiles(ids, gate_scales, up_scales, down_scales, gate, up, down):
    smem = pl.BlockSpec(memory_space=pltpu.SMEM)
    vmem = pl.BlockSpec(memory_space=pltpu.VMEM)
    return pl.pallas_call(
        tile_kernel,
        out_shape=jax.ShapeDtypeStruct((T, 3 * T), BF),
        in_specs=[smem] * 4 + [vmem] * 3,
        out_specs=vmem,
        name="own_tiles",
    )(ids, gate_scales, up_scales, down_scales, gate, up, down)


def forward_kernel(ids, tokens, out_grad, mine, theirs, own, p1, p2, p3, w_out, w_down):
    step = pl.program_id(0)
    z, core = ids[0], ids[1]

    @pl.when(step == 0)
    def _():
        for i in range(Z):
            base = (z ^ far_first(i)) * (2 * T)
            for ref, side in ((mine, core), (theirs, 1 - core)):
                rows = pl.ds(pl.multiple_of(base + side * T, T), T)
                w_out[rows, :] = ref[i * T : (i + 1) * T, 0 : 2 * T]
                w_down[rows, :] = ref[i * T : (i + 1) * T, 2 * T : 3 * T]

    gate_up = jnp.dot(tokens[...], w_out[...], preferred_element_type=F32)
    back = jnp.dot(out_grad[...], w_down[...], preferred_element_type=F32)

    @pl.when(step == 0)
    def _():
        own[:, 0 : 2 * T] = gate_up
        own[:, 2 * T : 3 * T] = back

    for k, ref in ((1, p1), (2, p2), (3, p3)):

        @pl.when(step == k)
        def _():
            ref[:, 0 : 2 * T] = gate_up.astype(BF)
            ref[:, 2 * T : 3 * T] = back.astype(BF)


def forward(ids, tokens, out_grad, mine, theirs):
    whole = lambda *shape: pl.BlockSpec(shape, lambda r, ids: (0,) * len(shape))
    rows = pl.BlockSpec((RB, D), lambda r, ids: (ids[2] ^ r, 0))
    part = jax.ShapeDtypeStruct((RB, 3 * T), BF)
    return pl.pallas_call(
        forward_kernel,
        grid_spec=pltpu.PrefetchScalarGridSpec(
            num_scalar_prefetch=1,
            grid=(XS,),
            in_specs=[rows, rows, whole(Z * T, 3 * T), whole(Z * T, 3 * T)],
            out_specs=[whole(RB, 3 * T)] * 4 + [whole(D, 2 * T)],
            scratch_shapes=[pltpu.VMEM((D, T), BF)],
        ),
        out_shape=[
            jax.ShapeDtypeStruct((RB, 3 * T), F32),
            part,
            part,
            part,
            jax.ShapeDtypeStruct((D, 2 * T), BF),
        ],
        compiler_params=pltpu.CompilerParams(
            dimension_semantics=("arbitrary",), vmem_limit_bytes=VMEM_LIMIT
        ),
        cost_estimate=pl.CostEstimate(
            flops=2 * CAP * D * 3 * T, bytes_accessed=12 * 1024 * 1024, transcendentals=0
        ),
        name="forward",
    )(ids, tokens, out_grad, mine, theirs)


def delta_kernel(s_mine, s_theirs, weight, out):
    total = s_mine[...].astype(F32) + s_theirs[...].astype(F32)
    gate, up, back = total[:, 0:T], total[:, T : 2 * T], total[:, 2 * T : 3 * T]
    s = jax.nn.sigmoid(gate)
    act = gate * s
    hidden_full = act * up
    delta = back * weight[...]
    out[0:RB, 0:T] = (delta * up * s * (1.0 + gate * (1.0 - s))).astype(BF)
    out[0:RB, T : 2 * T] = (delta * act).astype(BF)
    out[0:RB, 2 * T : 3 * T] = hidden_full.astype(BF)
    router = lax.dot_general(
        jnp.ones((8, T), F32),
        back * hidden_full,
        NT,
        precision=lax.Precision.HIGHEST,
        preferred_element_type=F32,
    )
    router = jnp.concatenate([router, jnp.zeros((8, 2 * T - RB), F32)], axis=1)
    hi = router.astype(BF).astype(F32)
    mid = (router - hi).astype(BF).astype(F32)
    low = router - hi - mid
    row = lax.broadcasted_iota(jnp.int32, (8, 2 * T), 0)
    pieces = jnp.where(row == 0, hi, jnp.where(row == 1, mid, jnp.where(row == 2, low, 0.0)))
    out[RB:MSG, 0 : 2 * T] = jnp.concatenate([pieces, jnp.zeros_like(pieces)], axis=0).astype(BF)
    out[RB:MSG, 2 * T : 3 * T] = jnp.zeros((16, T), BF)


def deltas(s_mine, s_theirs, weight):
    vmem = pl.BlockSpec(memory_space=pltpu.VMEM)
    return pl.pallas_call(
        delta_kernel,
        out_shape=jax.ShapeDtypeStruct((MSG, 3 * T), BF),
        in_specs=[vmem] * 3,
        out_specs=vmem,
        name="deltas",
    )(s_mine, s_theirs, weight)


def weight_grad_kernel(ids, tokens, out_grad, weight, d0, d1, d2, d3, keep, send, flat, turned):
    step = pl.program_id(0)
    core, x = ids[1], ids[2]

    @pl.when(step == 0)
    def _():
        for r, ref in enumerate((d0, d1, d2, d3)):
            rows = pl.ds(pl.multiple_of((x ^ r) * RB, RB), RB)
            flat[rows, :] = ref[0:RB, :]
        turned[...] = flat[...].astype(F32).T.astype(BF)

    scaled = (out_grad[...].astype(F32) * weight[...]).astype(BF)
    gate_up = jnp.dot(turned[0 : 2 * T, :], tokens[...], preferred_element_type=F32)
    down = jnp.dot(turned[2 * T : 3 * T, :], scaled, preferred_element_type=F32)
    for rows, value in ((slice(0, 2 * T), gate_up), (slice(2 * T, 3 * T), down)):
        low, high = value[:, 0:T].astype(BF), value[:, T : 2 * T].astype(BF)
        keep[rows, :] = jnp.where(core == 0, low, high)
        send[rows, :] = jnp.where(core == 0, high, low)


def weight_grads(ids, tokens, out_grad, weight, parts):
    whole = lambda *shape: pl.BlockSpec(shape, lambda i, ids: (0,) * len(shape))
    columns = pl.BlockSpec((CAP, 2 * T), lambda i, ids: (0, ids[0] ^ far_first(i)))
    block = pl.BlockSpec((3 * T, T), lambda i, ids: (i, 0))
    return pl.pallas_call(
        weight_grad_kernel,
        grid_spec=pltpu.PrefetchScalarGridSpec(
            num_scalar_prefetch=1,
            grid=(Z,),
            in_specs=[columns, columns, whole(CAP, 1)] + [whole(MSG, 3 * T)] * 4,
            out_specs=[block, block],
            scratch_shapes=[pltpu.VMEM((CAP, 3 * T), BF), pltpu.VMEM((3 * T, CAP), BF)],
        ),
        out_shape=[jax.ShapeDtypeStruct((Z * 3 * T, T), BF)] * 2,
        compiler_params=pltpu.CompilerParams(
            dimension_semantics=("arbitrary",), vmem_limit_bytes=VMEM_LIMIT
        ),
        cost_estimate=pl.CostEstimate(
            flops=2 * CAP * D * 3 * T, bytes_accessed=12 * 1024 * 1024, transcendentals=0
        ),
        name="weight_grads",
    )(ids, tokens, out_grad, weight, *parts)


def token_grad_kernel(ids, w0, near, far, y0, y1, y2, y3, out, flat):
    step = pl.program_id(0)
    x = ids[2]

    @pl.when(step == 0)
    def _():
        for j, ref in enumerate((y0, y1, y2, y3)):
            for r in range(XS):
                rows = pl.ds(pl.multiple_of((x ^ r) * RB, RB), RB)
                flat[rows, j * 2 * T : (j + 1) * 2 * T] = ref[r * MSG : r * MSG + RB, :]

    def total(ref):
        value = lax.dot_general(flat[:, 0 : 2 * T], w0[...], NT, preferred_element_type=F32)
        for j in range(3):
            value += lax.dot_general(
                flat[:, (j + 1) * 2 * T : (j + 2) * 2 * T],
                ref[j],
                NT,
                preferred_element_type=F32,
            )
        return value.astype(BF)

    @pl.when(step < Z // 2)
    def _():
        out[...] = total(near)

    @pl.when(step >= Z // 2)
    def _():
        out[...] = total(far)


def token_grads(ids, w_own, near, far, rows_by_y):
    whole = lambda *shape: pl.BlockSpec(shape, lambda i, ids: (0,) * len(shape))
    half = Z // 2
    at = lambda i, ids: lax.rem(ids[1] * half + i, Z)
    block = lambda index: pl.BlockSpec((3, 2 * T, 2 * T), lambda i, ids: (0, index(i), 0))
    return pl.pallas_call(
        token_grad_kernel,
        grid_spec=pltpu.PrefetchScalarGridSpec(
            num_scalar_prefetch=1,
            grid=(Z,),
            in_specs=[
                pl.BlockSpec((2 * T, 2 * T), lambda i, ids: (at(i, ids), 0)),
                block(lambda i: jnp.minimum(i, half - 1)),
                block(lambda i: jnp.maximum(i - half, 0)),
            ]
            + [whole(XS * MSG, 2 * T)] * 4,
            out_specs=pl.BlockSpec((CAP, 2 * T), lambda i, ids: (0, at(i, ids))),
            scratch_shapes=[pltpu.VMEM((CAP, 8 * T), BF)],
        ),
        out_shape=jax.ShapeDtypeStruct((CAP, D), BF),
        compiler_params=pltpu.CompilerParams(
            dimension_semantics=("arbitrary",), vmem_limit_bytes=VMEM_LIMIT
        ),
        cost_estimate=pl.CostEstimate(
            flops=2 * CAP * D * 8 * T, bytes_accessed=12 * 1024 * 1024, transcendentals=0
        ),
        name="token_grads",
    )(ids, w_own, near, far, *rows_by_y)


def local(
    tokens,
    out_grad,
    router_logits,
    routed_counts,
    routed_positions,
    gate_values,
    up_values,
    down_values,
    gate_scales,
    up_scales,
    down_scales,
):
    z, core, x = lax.axis_index("z"), lax.axis_index("core"), lax.axis_index("x")
    ids = jnp.stack([z, core, x]).astype(jnp.int32)

    held = own_tiles(ids, gate_scales, up_scales, down_scales, gate_values, up_values, down_values)
    for mask in (4, 2, 1):
        held = jnp.concatenate([held, swap(held, "z", Z, mask)], axis=0)
    held_other = swap(held, "core", CORES, 1)

    live = (jnp.arange(CAP) < routed_counts[0]).astype(F32)
    rate = jax.nn.sigmoid(jnp.take(router_logits, routed_positions))
    weight = rate * live
    weight_column = weight[:, None]
    weight_block = lax.dynamic_slice_in_dim(weight, x * RB, RB)[:, None]

    own, p1, p2, p3, w_own = forward(ids, tokens, out_grad, held, held_other)
    got = [swap(p, "x", XS, r) for r, p in ((1, p1), (2, p2), (3, p3))]
    total = own
    for g in got:
        total = total + g.astype(F32)
    total = total.astype(BF)
    total_other = swap(total, "zhi", Z_HI, 1)

    half = lax.dynamic_slice_in_dim(w_own, core * (D // 2), D // 2, axis=0)
    near = jnp.stack([swap(half, "row", ROWS, r) for r in (1, 2, 3)])
    far = swap(near, "core", CORES, 1)

    message = deltas(total, total_other, weight_block)
    parts = [message] + [swap(message, "x", XS, r) for r in (1, 2, 3)]

    keep, send = weight_grads(ids, tokens, out_grad, weight_column, parts)
    received = swap(send, "core", CORES, 1)
    sums = keep.astype(F32) + received.astype(F32)
    for mask, count in ((1, 4), (2, 2), (4, 1)):
        cut = count * 3 * T
        received = swap(sums[cut:].astype(BF), "z", Z, mask)
        sums = sums[:cut] + received.astype(F32)
    grad_gate = sums[0:T].T
    grad_up = sums[T : 2 * T].T
    grad_down = sums[2 * T : 3 * T]

    rows = jnp.concatenate([p[:, 0 : 2 * T] for p in parts], axis=0)
    rows_by_y = [rows] + [swap(rows, "row", ROWS, r) for r in (1, 2, 3)]
    grad_tokens = token_grads(ids, w_own, near, far, rows_by_y)

    def router_terms(block):
        pieces = block.reshape(XS, MSG, 2 * T)[:, RB : RB + 3, 0:RB].astype(F32)
        return pieces[:, 0] + pieces[:, 1] + pieces[:, 2]

    r0, r1, r2, r3 = (router_terms(block) for block in rows_by_y)
    router = (r0 + r1) + (r2 + r3)
    router = jnp.take(router, x ^ jnp.arange(XS), axis=0).reshape(CAP)
    logit_delta = router * rate * (1.0 - rate) * live
    grad_logits = jnp.zeros(router_logits.shape, F32).at[routed_positions].add(logit_delta)
    return (grad_tokens, grad_gate, grad_up, grad_down, grad_logits)


def solution(mesh):
    fine = Mesh(mesh.devices.reshape(Z, CORES, ROWS, Z_HI, XS), AXES)
    dp, col = ("z", "core"), ("zhi", "x")
    placed = (
        P(dp, col),
        P(dp, col),
        P(dp),
        P(dp),
        P(dp),
        P(col + dp, "row"),
        P(col + dp, "row"),
        P("row", col + dp),
        P(col, "row"),
        P(col, "row"),
        P("row", col),
    )
    return jax.shard_map(
        local,
        mesh=fine,
        in_specs=placed,
        out_specs=(P(dp, col), P(col + dp, "row"), P(col + dp, "row"), P("row", col + dp), P(dp)),
        check_vma=False,
    )
```

```python
import jax
import jax.numpy as jnp
from jax import lax
from jax.experimental import pallas as pl
from jax.experimental.pallas import tpu as pltpu
from jax.sharding import Mesh, PartitionSpec as P

BF = jnp.bfloat16
F32 = jnp.float32
Z, CORES, ROWS, Z_HI, XS = 8, 2, 4, 2, 4
T = 128
CAP = 768
SEQ = 6144
D = 2048
RB = CAP // XS
MSG = RB + 16
AXES = ("z", "core", "row", "zhi", "x")
NT = (((1,), (1,)), ((), ()))


def swap(value, axis, size, mask):
    return lax.ppermute(value, axis, [(i, i ^ mask) for i in range(size)])


def far_first(i):
    return ((i & 1) << 2) | (i & 2) | ((i >> 2) & 1)


def split3(value):
    hi = value.astype(BF)
    rest = value - hi.astype(F32)
    mid = rest.astype(BF)
    return hi, mid, (rest - mid.astype(F32)).astype(BF)


def params(mib=24):
    return pltpu.CompilerParams(
        dimension_semantics=("arbitrary",), vmem_limit_bytes=mib * 1024 * 1024
    )


def work(flops, mib):
    return pl.CostEstimate(flops=flops, bytes_accessed=mib * 1024 * 1024, transcendentals=0)


VMEM = pl.BlockSpec(memory_space=pltpu.VMEM)
SMEM = pl.BlockSpec(memory_space=pltpu.SMEM)
ANY = pl.BlockSpec(memory_space=pl.ANY)
HBM = pl.BlockSpec(memory_space=pltpu.HBM)


def turn(row):
    return jnp.broadcast_to(row, (8, row.shape[1])).T[:, 0:1]


def rates_kernel(logits, positions, counts, out):
    place = turn(positions[...].astype(F32))
    at = place.astype(jnp.int32)
    lanes = lax.broadcasted_iota(jnp.int32, (CAP, T), 1)
    upper = jnp.where(lanes[:, 0 : SEQ // T] == (at >> 7), 1.0, 0.0).astype(BF)
    picked = jnp.zeros((CAP, T), F32)
    for piece in split3(logits[...]):
        picked = picked + jnp.dot(upper, piece, preferred_element_type=F32)
    logit = jnp.sum(jnp.where(lanes == (at & (T - 1)), picked, 0.0), axis=1, keepdims=True)
    rate = jax.nn.sigmoid(logit)
    row = lax.broadcasted_iota(jnp.int32, (CAP, 1), 0)
    live = jnp.where(row < counts[0], 1.0, 0.0)
    weight = rate * live
    slope = rate * (1.0 - rate) * live
    out[...] = jnp.where(lanes == 0, weight, jnp.where(lanes == 1, slope, place))


def rates(logits, positions, counts):
    return pl.pallas_call(
        rates_kernel,
        out_shape=jax.ShapeDtypeStruct((CAP, T), F32),
        in_specs=[VMEM, VMEM, SMEM],
        out_specs=VMEM,
        name="rates",
    )(logits, positions, counts)


def tile_kernel(ids, gs, us, ds, gate, up, down, out):
    dp = ids[0] * CORES + ids[1]
    lane = lax.broadcasted_iota(jnp.int32, (1, Z * CORES), 1)
    g, u, d = (
        jnp.sum(jnp.where(lane == dp, ref[...], 0.0), axis=1, keepdims=True) for ref in (gs, us, ds)
    )
    out[:, 0:T] = (gate[...].astype(F32) * g).astype(BF)
    out[:, T : 2 * T] = (up[...].astype(F32) * u).astype(BF)
    out[:, 2 * T : 3 * T] = (down[...].astype(F32) * d).T.astype(BF)


def own_tiles(ids, gate_scales, up_scales, down_scales, gate, up, down):
    return pl.pallas_call(
        tile_kernel,
        out_shape=jax.ShapeDtypeStruct((T, 3 * T), BF),
        in_specs=[SMEM] + [VMEM] * 6,
        out_specs=VMEM,
        name="own_tiles",
    )(ids, gate_scales, up_scales, down_scales, gate, up, down)


def forward_kernel(
    ids, tokens, out_grad, m0, m1, t0, t1, after, own, p1, p2, p3, w_out, half, w_down, rows_in, sems
):
    step = pl.program_id(0)
    z, core, x = ids[0], ids[1], ids[2]

    def fetch(k, r):
        source = (tokens, out_grad)[k].at[pl.ds(pl.multiple_of((x ^ r) * RB, RB), RB), :]
        return pltpu.make_async_copy(source, rows_in.at[k, r], sems.at[k, r])

    @pl.when(step == 0)
    def _():
        for r in range(XS):
            for k in range(2):
                fetch(k, r).start()
        for i in range(Z):
            base = (z ^ far_first(i)) * (2 * T)
            for pair, side in (((m0, m1), core), ((t0, t1), 1 - core)):
                ref, j = pair[i // 4], i % 4
                rows = pl.ds(pl.multiple_of(base + side * T, T), T)
                w_out[rows, :] = ref[j * T : (j + 1) * T, 0 : 2 * T]
                w_down[rows, :] = ref[j * T : (j + 1) * T, 2 * T : 3 * T]

        half[0 : 4 * T, :] = m0[:, 0 : 2 * T]
        half[4 * T : 8 * T, :] = m1[:, 0 : 2 * T]

    fetch(0, step).wait()
    gate_up = jnp.dot(rows_in[0, step], w_out[...], preferred_element_type=F32)
    fetch(1, step).wait()
    back = jnp.dot(rows_in[1, step], w_down[...], preferred_element_type=F32)

    @pl.when(step == 0)
    def _():
        own[:, 0 : 2 * T] = gate_up
        own[:, 2 * T : 3 * T] = back

    for k, ref in ((1, p1), (2, p2), (3, p3)):

        @pl.when(step == k)
        def _():
            ref[:, 0 : 2 * T] = gate_up.astype(BF)
            ref[:, 2 * T : 3 * T] = back.astype(BF)


def forward(ids, tokens, out_grad, mine, theirs, after):
    whole = lambda *shape: pl.BlockSpec(shape, lambda r, ids: (0,) * len(shape))
    part = jax.ShapeDtypeStruct((RB, 3 * T), BF)
    return pl.pallas_call(
        forward_kernel,
        grid_spec=pltpu.PrefetchScalarGridSpec(
            num_scalar_prefetch=1,
            grid=(XS,),
            in_specs=[HBM, HBM] + [whole(4 * T, 3 * T)] * 4 + [ANY],
            out_specs=[whole(RB, 3 * T)] * 4 + [whole(D, 2 * T), whole(8 * T, 2 * T)],
            scratch_shapes=[
                pltpu.VMEM((D, T), BF),
                pltpu.VMEM((2, XS, RB, D), BF),
                pltpu.SemaphoreType.DMA((2, XS)),
            ],
        ),
        out_shape=[
            jax.ShapeDtypeStruct((RB, 3 * T), F32),
            part,
            part,
            part,
            jax.ShapeDtypeStruct((D, 2 * T), BF),
            jax.ShapeDtypeStruct((8 * T, 2 * T), BF),
        ],
        compiler_params=params(56),
        cost_estimate=work(2 * CAP * D * 3 * T, 10),
        name="forward",
    )(ids, tokens, out_grad, *mine, *theirs, after)


def reduce_kernel(own, g1, g2, g3, total):
    total[...] = (
        own[...] + g1[...].astype(F32) + g2[...].astype(F32) + g3[...].astype(F32)
    ).astype(BF)


def reduce_rows(own, got):
    return pl.pallas_call(
        reduce_kernel,
        out_shape=jax.ShapeDtypeStruct((RB, 3 * T), BF),
        in_specs=[VMEM] * 4,
        out_specs=VMEM,
        name="reduce_rows",
    )(own, *got)


def collect_kernel(*refs):
    n = len(refs) - 3
    out, sems = refs[-2], refs[-1]
    copies = [pltpu.make_async_copy(refs[i], out.at[i], sems.at[i]) for i in range(n)]
    for copy in copies:
        copy.start()
    for copy in copies:
        copy.wait()


def collect(arrays, after):
    n = len(arrays)
    return pl.pallas_call(
        collect_kernel,
        out_shape=jax.ShapeDtypeStruct((n,) + arrays[0].shape, arrays[0].dtype),
        in_specs=[ANY] * (n + 1),
        out_specs=ANY,
        scratch_shapes=[pltpu.SemaphoreType.DMA((n,))],
        name="collect",
    )(*arrays, after)


def delta_kernel(ids, s_mine, s_theirs, per_row, out):
    total = s_mine[...].astype(F32) + s_theirs[...].astype(F32)
    gate, up, back = total[:, 0:T], total[:, T : 2 * T], total[:, 2 * T : 3 * T]
    weight = per_row[pl.ds(pl.multiple_of(ids[2] * RB, RB), RB), :][:, 0:1]
    s = jax.nn.sigmoid(gate)
    act = gate * s
    hidden_full = act * up
    delta = back * weight
    out[0:RB, 0:T] = (delta * up * s * (1.0 + gate * (1.0 - s))).astype(BF)
    out[0:RB, T : 2 * T] = (delta * act).astype(BF)
    out[0:RB, 2 * T : 3 * T] = hidden_full.astype(BF)
    router = lax.dot_general(
        jnp.ones((8, T), F32),
        back * hidden_full,
        NT,
        precision=lax.Precision.HIGHEST,
        preferred_element_type=F32,
    )
    router = jnp.concatenate([router, jnp.zeros((8, 2 * T - RB), F32)], axis=1)
    hi, mid, low = (piece.astype(F32) for piece in split3(router))
    row = lax.broadcasted_iota(jnp.int32, (8, 2 * T), 0)
    pieces = jnp.where(row == 0, hi, jnp.where(row == 1, mid, jnp.where(row == 2, low, 0.0)))
    out[RB:MSG, 0 : 2 * T] = jnp.concatenate([pieces, jnp.zeros_like(pieces)], axis=0).astype(BF)
    out[RB:MSG, 2 * T : 3 * T] = jnp.zeros((16, T), BF)


def deltas(ids, s_mine, s_theirs, per_row):
    return pl.pallas_call(
        delta_kernel,
        out_shape=jax.ShapeDtypeStruct((MSG, 3 * T), BF),
        in_specs=[SMEM] + [VMEM] * 3,
        out_specs=VMEM,
        name="deltas",
    )(ids, s_mine, s_theirs, per_row)


def weight_grad_kernel(
    ids,
    tokens,
    out_grad,
    per_row,
    d0,
    d1,
    d2,
    d3,
    a,
    b,
    c,
    keep,
    send,
    flat,
    turned,
    columns_in,
    sems,
):
    step = pl.program_id(0)
    z, core, x = ids[0], ids[1], ids[2]

    def fetch(k, i):
        columns = pl.ds(pl.multiple_of((z ^ far_first(i ^ 4)) * (2 * T), 2 * T), 2 * T)
        source = (tokens, out_grad)[k].at[:, columns]
        return pltpu.make_async_copy(source, columns_in.at[k, i], sems.at[k, i])

    @pl.when(step == 0)
    def _():
        for i in range(Z):
            for k in range(2):
                fetch(k, i).start()
        for r, ref in enumerate((d0, d1, d2, d3)):
            rows = pl.ds(pl.multiple_of((x ^ r) * RB, RB), RB)
            flat[rows, :] = ref[0:RB, :]
        turned[...] = flat[...].astype(F32).T.astype(BF)

    fetch(0, step).wait()
    gate_up = jnp.dot(turned[0 : 2 * T, :], columns_in[0, step], preferred_element_type=F32)
    fetch(1, step).wait()
    scaled = (columns_in[1, step].astype(F32) * per_row[:, 0:1]).astype(BF)
    down = jnp.dot(turned[2 * T : 3 * T, :], scaled, preferred_element_type=F32)
    for rows, value in ((slice(0, 2 * T), gate_up), (slice(2 * T, 3 * T), down)):
        low, high = value[:, 0:T].astype(BF), value[:, T : 2 * T].astype(BF)
        keep[rows, :] = jnp.where(core == 0, low, high)
        send[rows, :] = jnp.where(core == 0, high, low)


def weight_grads(ids, tokens, out_grad, per_row, parts, after):
    whole = lambda *shape: pl.BlockSpec(shape, lambda i, ids: (0,) * len(shape))
    block = pl.BlockSpec((3 * T, T), lambda i, ids: (i, 0))
    return pl.pallas_call(
        weight_grad_kernel,
        grid_spec=pltpu.PrefetchScalarGridSpec(
            num_scalar_prefetch=1,
            grid=(Z,),
            in_specs=[HBM, HBM, whole(CAP, T)] + [whole(MSG, 3 * T)] * 4 + [ANY] * 3,
            out_specs=[block, block],
            scratch_shapes=[
                pltpu.VMEM((CAP, 3 * T), BF),
                pltpu.VMEM((3 * T, CAP), BF),
                pltpu.VMEM((2, Z, CAP, 2 * T), BF),
                pltpu.SemaphoreType.DMA((2, Z)),
            ],
        ),
        out_shape=[jax.ShapeDtypeStruct((Z * 3 * T, T), BF)] * 2,
        compiler_params=params(),
        cost_estimate=work(2 * CAP * D * 3 * T, 10),
        name="weight_grads",
    )(ids, tokens, out_grad, per_row, *parts, *after)


def core_sum_kernel(keep, received, send):
    rows = slice(0, 4 * 3 * T)
    send[...] = (keep[rows, :].astype(F32) + received[rows, :].astype(F32)).astype(BF)


def core_sum(keep, received):
    return pl.pallas_call(
        core_sum_kernel,
        out_shape=jax.ShapeDtypeStruct((4 * 3 * T, T), BF),
        in_specs=[VMEM] * 2,
        out_specs=VMEM,
        name="core_sum",
    )(keep, received)


def rows_kernel(ids, d0, d1, d2, d3, after, rows_out):
    x = ids[2]
    for r, ref in enumerate((d0, d1, d2, d3)):
        rows = pl.ds(pl.multiple_of((x ^ r) * RB, RB), RB)
        rows_out[rows, :] = ref[0:RB, 0 : 2 * T]
        rows_out[CAP + 16 * r : CAP + 16 * (r + 1), :] = ref[RB:MSG, 0 : 2 * T]


def row_order(ids, parts, after):
    return pl.pallas_call(
        rows_kernel,
        out_shape=jax.ShapeDtypeStruct((CAP + XS * 16, 2 * T), BF),
        in_specs=[SMEM] + [VMEM] * 4 + [ANY],
        out_specs=VMEM,
        name="row_order",
    )(ids, *parts, after)


def pair_sum_kernel(keep, received, arrived, y1, y3, own, s4, s2, s6):
    for i, out in enumerate((own, s4, s2, s6)):
        there = slice(i * 3 * T, (i + 1) * 3 * T)
        here = slice((i + 4) * 3 * T, (i + 5) * 3 * T)
        total = keep[here, :].astype(F32) + received[here, :].astype(F32)
        out[...] = (total + arrived[there, :].astype(F32)).astype(out.dtype)


def pair_sum(keep, received, arrived, after):
    part = jax.ShapeDtypeStruct((3 * T, T), BF)
    return pl.pallas_call(
        pair_sum_kernel,
        out_shape=[jax.ShapeDtypeStruct((3 * T, T), F32), part, part, part],
        in_specs=[VMEM] * 3 + [ANY] * 2,
        out_specs=[VMEM] * 4,
        name="pair_sum",
    )(keep, received, arrived, *after)


def last_sum_kernel(own, r4, r2, r6, after, gate, up, down):
    total = own[...] + r4[...].astype(F32) + r2[...].astype(F32) + r6[...].astype(F32)
    gate[...] = total[0:T].T
    up[...] = total[T : 2 * T].T
    down[...] = total[2 * T : 3 * T]


def last_sum(own, r4, r2, r6, after):
    return pl.pallas_call(
        last_sum_kernel,
        out_shape=[jax.ShapeDtypeStruct((T, T), F32)] * 3,
        in_specs=[VMEM] * 4 + [ANY],
        out_specs=[VMEM] * 3,
        name="last_sum",
    )(own, r4, r2, r6, after)


def token_grad_kernel(
    ids, w0, near, far, y0, y1, y2, y3, per_row, after, out, logits_out, w, router
):
    step = pl.program_id(0)
    core, x = ids[1], ids[2]

    @pl.when(step == 0)
    def _():
        for r in range(XS):
            rows = slice(CAP + 16 * r, CAP + 16 * (r + 1))
            terms = []
            for ref in (y0, y1, y2, y3):
                pieces = ref[rows, :].astype(F32)
                terms.append(pieces[0:1] + pieces[1:2] + pieces[2:3])
            total = (terms[0] + terms[1]) + (terms[2] + terms[3])
            router[pl.ds(pl.multiple_of((x ^ r) * RB, RB), RB), :] = turn(total)[0:RB]
        value = router[...] * per_row[:, 1:2]
        at = per_row[:, 2:3].astype(jnp.int32)
        lanes = lax.broadcasted_iota(jnp.int32, (CAP, T), 1)
        upper = jnp.where(lanes == (at >> 7), 1.0, 0.0).T.astype(BF)
        spread = jnp.where(lanes == (at & (T - 1)), value, 0.0)
        total = jnp.zeros((T, T), F32)
        for piece in split3(spread):
            total = total + jnp.dot(upper, piece, preferred_element_type=F32)
        logits_out[...] = total[0 : SEQ // T, :]

    mine = pl.ds(pl.multiple_of(core * T, T), T)
    theirs = pl.ds(pl.multiple_of((1 - core) * T, T), T)
    total = lax.dot_general(y0[0:CAP, :], w0[...], NT, preferred_element_type=F32)
    for j, ref in enumerate((y1, y2, y3)):
        w[j, mine, :] = near[j]
        w[j, theirs, :] = far[j]
        total = total + lax.dot_general(ref[0:CAP, :], w[j], NT, preferred_element_type=F32)
    out[...] = total.astype(BF)


def token_grads(ids, w_own, near, far, rows_by_y, per_row, after):
    whole = lambda *shape: pl.BlockSpec(shape, lambda i, ids: (0,) * len(shape))
    zb = lambda i, ids: ids[0] ^ far_first(i)
    tiles = pl.BlockSpec((3, T, 2 * T), lambda i, ids: (0, i, 0))
    return pl.pallas_call(
        token_grad_kernel,
        grid_spec=pltpu.PrefetchScalarGridSpec(
            num_scalar_prefetch=1,
            grid=(Z,),
            in_specs=[pl.BlockSpec((2 * T, 2 * T), lambda i, ids: (zb(i, ids), 0)), tiles, tiles]
            + [whole(CAP + XS * 16, 2 * T)] * 4
            + [whole(CAP, T), ANY],
            out_specs=[
                pl.BlockSpec((CAP, 2 * T), lambda i, ids: (0, zb(i, ids))),
                whole(SEQ // T, T),
            ],
            scratch_shapes=[pltpu.VMEM((3, 2 * T, 2 * T), BF), pltpu.VMEM((CAP, 1), F32)],
        ),
        out_shape=[
            jax.ShapeDtypeStruct((CAP, D), BF),
            jax.ShapeDtypeStruct((SEQ // T, T), F32),
        ],
        compiler_params=params(),
        cost_estimate=work(2 * CAP * D * 8 * T, 12),
        name="token_grads",
    )(ids, w_own, near, far, *rows_by_y, per_row, after)


def local(
    tokens,
    out_grad,
    router_logits,
    routed_counts,
    routed_positions,
    gate_values,
    up_values,
    down_values,
    gate_scales,
    up_scales,
    down_scales,
):
    z, core, x = lax.axis_index("z"), lax.axis_index("core"), lax.axis_index("x")
    ids = jnp.stack([z, core, x]).astype(jnp.int32)

    scales = (gate_scales.T, up_scales.T, down_scales)
    held = own_tiles(ids, *scales, gate_values, up_values, down_values)
    held = jnp.concatenate([held] + [swap(held, "z", Z, mask) for mask in (4, 2, 6)], axis=0)
    mine = (held, swap(held, "z", Z, 1))
    theirs = tuple(swap(h, "core", CORES, 1) for h in mine)
    per_row = rates(router_logits.reshape(SEQ // T, T), routed_positions[None, :], routed_counts)

    own, p1, p2, p3, w_own, half = forward(ids, tokens, out_grad, mine, theirs, per_row)
    got = [swap(p, "x", XS, r) for r, p in ((1, p1), (2, p2), (3, p3))]
    total = reduce_rows(own, got)
    message = deltas(ids, total, swap(total, "zhi", Z_HI, 1), per_row)
    parts = [message] + [swap(message, "x", XS, r) for r in (1, 2, 3)]

    half = collect([half], total)[0]
    by_y = [swap(half, "row", ROWS, r) for r in (1, 2, 3)]

    keep, send = weight_grads(ids, tokens, out_grad, per_row, parts, by_y)
    received = swap(send, "core", CORES, 1)
    arrived = swap(core_sum(keep, received), "z", Z, 1)

    rows = row_order(ids, parts, keep)
    y1, y2, y3 = (swap(rows, "row", ROWS, r) for r in (1, 2, 3))
    own_sum, s4, s2, s6 = pair_sum(keep, received, arrived, (y1, y3))
    near = collect(by_y, s4)
    far = swap(near, "core", CORES, 1)
    grad_tokens, grad_logits = token_grads(
        ids, w_own, near, far, (rows, y1, y2, y3), per_row, s4
    )
    grad_gate, grad_up, grad_down = last_sum(
        own_sum,
        swap(s4, "z", Z, 4),
        swap(s2, "z", Z, 2),
        swap(s6, "z", Z, 6),
        grad_logits,
    )
    return (grad_tokens, grad_gate, grad_up, grad_down, grad_logits.reshape(SEQ))


def solution(mesh):
    fine = Mesh(mesh.devices.reshape(Z, CORES, ROWS, Z_HI, XS), AXES)
    dp, col = ("z", "core"), ("zhi", "x")
    placed = (
        P(dp, col),
        P(dp, col),
        P(dp),
        P(dp),
        P(dp),
        P(col + dp, "row"),
        P(col + dp, "row"),
        P("row", col + dp),
        P(col, "row"),
        P(col, "row"),
        P("row", col),
    )
    return jax.shard_map(
        local,
        mesh=fine,
        in_specs=placed,
        out_specs=(P(dp, col), P(col + dp, "row"), P(col + dp, "row"), P("row", col + dp), P(dp)),
        check_vma=False,
    )
```

```python
import jax
import jax.numpy as jnp
from jax import lax
from jax.experimental import pallas as pl
from jax.experimental.pallas import tpu as pltpu
from jax.sharding import Mesh, PartitionSpec as P

BF = jnp.bfloat16
F32 = jnp.float32
Z, CORES, ROWS, Z_HI, XS = 8, 2, 4, 2, 4
T = 128
CAP = 768
SEQ = 6144
D = 2048
RB = CAP // XS
MSG = RB + 16
AXES = ("z", "core", "row", "zhi", "x")
NT = (((1,), (1,)), ((), ()))


def swap(value, axis, size, mask):
    return lax.ppermute(value, axis, [(i, i ^ mask) for i in range(size)])


def far_first(i):
    return ((i & 1) << 2) | (i & 2) | ((i >> 2) & 1)


def split3(value):
    hi = value.astype(BF)
    rest = value - hi.astype(F32)
    mid = rest.astype(BF)
    return hi, mid, (rest - mid.astype(F32)).astype(BF)


def params(mib=44):
    return pltpu.CompilerParams(
        dimension_semantics=("arbitrary",), vmem_limit_bytes=mib * 1024 * 1024
    )


def work(flops, mib):
    return pl.CostEstimate(flops=flops, bytes_accessed=mib * 1024 * 1024, transcendentals=0)


VMEM = pl.BlockSpec(memory_space=pltpu.VMEM)
SMEM = pl.BlockSpec(memory_space=pltpu.SMEM)
ANY = pl.BlockSpec(memory_space=pl.ANY)
HBM = pl.BlockSpec(memory_space=pltpu.HBM)


def turn(row):
    return jnp.broadcast_to(row, (8, row.shape[1])).T[:, 0:1]


def rates_kernel(logits, positions, counts, out):
    place = turn(positions[...].astype(F32))
    at = place.astype(jnp.int32)
    lanes = lax.broadcasted_iota(jnp.int32, (CAP, T), 1)
    upper = jnp.where(lanes[:, 0 : SEQ // T] == (at >> 7), 1.0, 0.0).astype(BF)
    picked = jnp.zeros((CAP, T), F32)
    for piece in split3(logits[...]):
        picked = picked + jnp.dot(upper, piece, preferred_element_type=F32)
    logit = jnp.sum(jnp.where(lanes == (at & (T - 1)), picked, 0.0), axis=1, keepdims=True)
    rate = jax.nn.sigmoid(logit)
    row = lax.broadcasted_iota(jnp.int32, (CAP, 1), 0)
    live = jnp.where(row < counts[0], 1.0, 0.0)
    weight = rate * live
    slope = rate * (1.0 - rate) * live
    out[...] = jnp.where(lanes == 0, weight, jnp.where(lanes == 1, slope, place))


def rates(logits, positions, counts):
    return pl.pallas_call(
        rates_kernel,
        out_shape=jax.ShapeDtypeStruct((CAP, T), F32),
        in_specs=[VMEM, VMEM, SMEM],
        out_specs=VMEM,
        name="rates",
    )(logits, positions, counts)


def tile_kernel(ids, gs, us, ds, gate, up, down, out):
    dp = ids[0] * CORES + ids[1]
    lane = lax.broadcasted_iota(jnp.int32, (1, Z * CORES), 1)
    g, u, d = (
        jnp.sum(jnp.where(lane == dp, ref[...], 0.0), axis=1, keepdims=True) for ref in (gs, us, ds)
    )
    out[:, 0:T] = (gate[...].astype(F32) * g).astype(BF)
    out[:, T : 2 * T] = (up[...].astype(F32) * u).astype(BF)
    out[:, 2 * T : 3 * T] = (down[...].astype(F32) * d).T.astype(BF)


def own_tiles(ids, gate_scales, up_scales, down_scales, gate, up, down):
    return pl.pallas_call(
        tile_kernel,
        out_shape=jax.ShapeDtypeStruct((T, 3 * T), BF),
        in_specs=[SMEM] + [VMEM] * 6,
        out_specs=VMEM,
        name="own_tiles",
    )(ids, gate_scales, up_scales, down_scales, gate, up, down)


def forward_kernel(ids, tokens, out_grad, m0, m1, t0, t1, own, p1, p2, p3, w_out, w_down):
    step = pl.program_id(0)
    z, core = ids[0], ids[1]

    @pl.when(step == 0)
    def _():
        for i in range(Z):
            base = (z ^ far_first(i)) * (2 * T)
            for pair, side in (((m0, m1), core), ((t0, t1), 1 - core)):
                ref, j = pair[i // 4], i % 4
                rows = pl.ds(pl.multiple_of(base + side * T, T), T)
                w_out[rows, :] = ref[j * T : (j + 1) * T, 0 : 2 * T]
                w_down[rows, :] = ref[j * T : (j + 1) * T, 2 * T : 3 * T]

    gate_up = jnp.dot(tokens[...], w_out[...], preferred_element_type=F32)
    back = jnp.dot(out_grad[...], w_down[...], preferred_element_type=F32)

    @pl.when(step == 0)
    def _():
        own[:, 0 : 2 * T] = gate_up
        own[:, 2 * T : 3 * T] = back

    for k, ref in ((1, p1), (2, p2), (3, p3)):

        @pl.when(step == k)
        def _():
            ref[:, 0 : 2 * T] = gate_up.astype(BF)
            ref[:, 2 * T : 3 * T] = back.astype(BF)


def forward(ids, tokens, out_grad, mine, theirs):
    whole = lambda *shape: pl.BlockSpec(shape, lambda r, ids: (0,) * len(shape))
    rows = pl.BlockSpec((RB, D), lambda r, ids: (ids[2] ^ r, 0))
    part = jax.ShapeDtypeStruct((RB, 3 * T), BF)
    return pl.pallas_call(
        forward_kernel,
        grid_spec=pltpu.PrefetchScalarGridSpec(
            num_scalar_prefetch=1,
            grid=(XS,),
            in_specs=[rows, rows] + [whole(4 * T, 3 * T)] * 4,
            out_specs=[whole(RB, 3 * T)] * 4 + [whole(D, 2 * T)],
            scratch_shapes=[pltpu.VMEM((D, T), BF)],
        ),
        out_shape=[
            jax.ShapeDtypeStruct((RB, 3 * T), F32),
            part,
            part,
            part,
            jax.ShapeDtypeStruct((D, 2 * T), BF),
        ],
        compiler_params=params(),
        cost_estimate=work(2 * CAP * D * 3 * T, 10),
        name="forward",
    )(ids, tokens, out_grad, *mine, *theirs)


def reduce_kernel(own, g1, g2, g3, total):
    total[...] = (
        own[...] + g1[...].astype(F32) + g2[...].astype(F32) + g3[...].astype(F32)
    ).astype(BF)


def reduce_rows(own, got):
    return pl.pallas_call(
        reduce_kernel,
        out_shape=jax.ShapeDtypeStruct((RB, 3 * T), BF),
        in_specs=[VMEM] * 4,
        out_specs=VMEM,
        name="reduce_rows",
    )(own, *got)


def delta_kernel(ids, s_mine, s_theirs, per_row, out):
    total = s_mine[...].astype(F32) + s_theirs[...].astype(F32)
    gate, up, back = total[:, 0:T], total[:, T : 2 * T], total[:, 2 * T : 3 * T]
    weight = per_row[pl.ds(pl.multiple_of(ids[2] * RB, RB), RB), :][:, 0:1]
    s = jax.nn.sigmoid(gate)
    act = gate * s
    hidden_full = act * up
    delta = back * weight
    out[0:RB, 0:T] = (delta * up * s * (1.0 + gate * (1.0 - s))).astype(BF)
    out[0:RB, T : 2 * T] = (delta * act).astype(BF)
    out[0:RB, 2 * T : 3 * T] = hidden_full.astype(BF)
    router = lax.dot_general(
        jnp.ones((8, T), F32),
        back * hidden_full,
        NT,
        precision=lax.Precision.HIGHEST,
        preferred_element_type=F32,
    )
    router = jnp.concatenate([router, jnp.zeros((8, 2 * T - RB), F32)], axis=1)
    hi, mid, low = (piece.astype(F32) for piece in split3(router))
    row = lax.broadcasted_iota(jnp.int32, (8, 2 * T), 0)
    pieces = jnp.where(row == 0, hi, jnp.where(row == 1, mid, jnp.where(row == 2, low, 0.0)))
    out[RB:MSG, 0 : 2 * T] = jnp.concatenate([pieces, jnp.zeros_like(pieces)], axis=0).astype(BF)
    out[RB:MSG, 2 * T : 3 * T] = jnp.zeros((16, T), BF)


def deltas(ids, s_mine, s_theirs, per_row):
    return pl.pallas_call(
        delta_kernel,
        out_shape=jax.ShapeDtypeStruct((MSG, 3 * T), BF),
        in_specs=[SMEM] + [VMEM] * 3,
        out_specs=VMEM,
        name="deltas",
    )(ids, s_mine, s_theirs, per_row)


def weight_grad_kernel(ids, tokens, out_grad, per_row, d0, d1, d2, d3, keep, send, flat, turned):
    step = pl.program_id(0)
    core, x = ids[1], ids[2]

    @pl.when(step == 0)
    def _():
        for r, ref in enumerate((d0, d1, d2, d3)):
            rows = pl.ds(pl.multiple_of((x ^ r) * RB, RB), RB)
            flat[rows, :] = ref[0:RB, :]
        turned[...] = flat[...].astype(F32).T.astype(BF)

    scaled = (out_grad[...].astype(F32) * per_row[:, 0:1]).astype(BF)
    gate_up = jnp.dot(turned[0 : 2 * T, :], tokens[...], preferred_element_type=F32)
    down = jnp.dot(turned[2 * T : 3 * T, :], scaled, preferred_element_type=F32)
    for rows, value in ((slice(0, 2 * T), gate_up), (slice(2 * T, 3 * T), down)):
        low, high = value[:, 0:T].astype(BF), value[:, T : 2 * T].astype(BF)
        keep[rows, :] = jnp.where(core == 0, low, high)
        send[rows, :] = jnp.where(core == 0, high, low)


def weight_grads(ids, tokens, out_grad, per_row, parts):
    whole = lambda *shape: pl.BlockSpec(shape, lambda i, ids: (0,) * len(shape))
    columns = pl.BlockSpec((CAP, 2 * T), lambda i, ids: (0, ids[0] ^ far_first(i ^ 4)))
    block = pl.BlockSpec((3 * T, T), lambda i, ids: (i, 0))
    return pl.pallas_call(
        weight_grad_kernel,
        grid_spec=pltpu.PrefetchScalarGridSpec(
            num_scalar_prefetch=1,
            grid=(Z,),
            in_specs=[columns, columns, whole(CAP, T)] + [whole(MSG, 3 * T)] * 4,
            out_specs=[block, block],
            scratch_shapes=[pltpu.VMEM((CAP, 3 * T), BF), pltpu.VMEM((3 * T, CAP), BF)],
        ),
        out_shape=[jax.ShapeDtypeStruct((Z * 3 * T, T), BF)] * 2,
        compiler_params=params(),
        cost_estimate=work(2 * CAP * D * 3 * T, 10),
        name="weight_grads",
    )(ids, tokens, out_grad, per_row, *parts)


def core_sum_kernel(keep, received, send):
    rows = slice(0, 4 * 3 * T)
    send[...] = (keep[rows, :].astype(F32) + received[rows, :].astype(F32)).astype(BF)


def core_sum(keep, received):
    return pl.pallas_call(
        core_sum_kernel,
        out_shape=jax.ShapeDtypeStruct((4 * 3 * T, T), BF),
        in_specs=[VMEM] * 2,
        out_specs=VMEM,
        name="core_sum",
    )(keep, received)


def rows_kernel(ids, d0, d1, d2, d3, after, rows_out):
    x = ids[2]
    for r, ref in enumerate((d0, d1, d2, d3)):
        rows = pl.ds(pl.multiple_of((x ^ r) * RB, RB), RB)
        rows_out[rows, :] = ref[0:RB, 0 : 2 * T]
        rows_out[CAP + 16 * r : CAP + 16 * (r + 1), :] = ref[RB:MSG, 0 : 2 * T]


def row_order(ids, parts, after):
    return pl.pallas_call(
        rows_kernel,
        out_shape=jax.ShapeDtypeStruct((CAP + XS * 16, 2 * T), BF),
        in_specs=[SMEM] + [VMEM] * 4 + [ANY],
        out_specs=VMEM,
        name="row_order",
    )(ids, *parts, after)


def pair_sum_kernel(keep, received, arrived, own, s4, s2, s6):
    for i, out in enumerate((own, s4, s2, s6)):
        there = slice(i * 3 * T, (i + 1) * 3 * T)
        here = slice((i + 4) * 3 * T, (i + 5) * 3 * T)
        total = keep[here, :].astype(F32) + received[here, :].astype(F32)
        out[...] = (total + arrived[there, :].astype(F32)).astype(out.dtype)


def pair_sum(keep, received, arrived):
    part = jax.ShapeDtypeStruct((3 * T, T), BF)
    return pl.pallas_call(
        pair_sum_kernel,
        out_shape=[jax.ShapeDtypeStruct((3 * T, T), F32), part, part, part],
        in_specs=[VMEM] * 3,
        out_specs=[VMEM] * 4,
        name="pair_sum",
    )(keep, received, arrived)


def last_sum_kernel(own, r4, r2, r6, after, gate, up, down):
    total = own[...] + r4[...].astype(F32) + r2[...].astype(F32) + r6[...].astype(F32)
    gate[...] = total[0:T].T
    up[...] = total[T : 2 * T].T
    down[...] = total[2 * T : 3 * T]


def last_sum(own, r4, r2, r6, after):
    return pl.pallas_call(
        last_sum_kernel,
        out_shape=[jax.ShapeDtypeStruct((T, T), F32)] * 3,
        in_specs=[VMEM] * 4 + [ANY],
        out_specs=[VMEM] * 3,
        name="last_sum",
    )(own, r4, r2, r6, after)


def token_grad_kernel(
    ids, weights, rows_by_y, per_row, after, out, logits_out, router
):
    step = pl.program_id(0)
    x = ids[2]

    @pl.when(step == 0)
    def _():
        for r in range(XS):
            rows = slice(CAP + 16 * r, CAP + 16 * (r + 1))
            terms = []
            for j in range(ROWS):
                pieces = rows_by_y[j, rows, :].astype(F32)
                terms.append(pieces[0:1] + pieces[1:2] + pieces[2:3])
            total = (terms[0] + terms[1]) + (terms[2] + terms[3])
            router[pl.ds(pl.multiple_of((x ^ r) * RB, RB), RB), :] = turn(total)[0:RB]
        value = router[...] * per_row[:, 1:2]
        at = per_row[:, 2:3].astype(jnp.int32)
        lanes = lax.broadcasted_iota(jnp.int32, (CAP, T), 1)
        upper = jnp.where(lanes == (at >> 7), 1.0, 0.0).T.astype(BF)
        spread = jnp.where(lanes == (at & (T - 1)), value, 0.0)
        total = jnp.zeros((T, T), F32)
        for piece in split3(spread):
            total = total + jnp.dot(upper, piece, preferred_element_type=F32)
        logits_out[...] = total[0 : SEQ // T, :]

    total = jnp.zeros((CAP, 2 * T), F32)
    for j in range(ROWS):
        total += lax.dot_general(
            rows_by_y[j, 0:CAP, :], weights[j], NT, preferred_element_type=F32
        )
    out[...] = total.astype(BF)


def token_grads(ids, weights, rows_by_y, per_row, after):
    whole = lambda *shape: pl.BlockSpec(shape, lambda i, ids: (0,) * len(shape))
    return pl.pallas_call(
        token_grad_kernel,
        grid_spec=pltpu.PrefetchScalarGridSpec(
            num_scalar_prefetch=1,
            grid=(Z,),
            in_specs=[
                pl.BlockSpec((ROWS, 2 * T, 2 * T), lambda i, ids: (0, i, 0)),
                whole(ROWS, CAP + XS * 16, 2 * T),
                whole(CAP, T),
                ANY,
            ],
            out_specs=[
                pl.BlockSpec((CAP, 2 * T), lambda i, ids: (0, i)),
                whole(SEQ // T, T),
            ],
            scratch_shapes=[pltpu.VMEM((CAP, 1), F32)],
        ),
        out_shape=[
            jax.ShapeDtypeStruct((CAP, D), BF),
            jax.ShapeDtypeStruct((SEQ // T, T), F32),
        ],
        compiler_params=params(),
        cost_estimate=work(2 * CAP * D * 8 * T, 12),
        name="token_grads",
    )(ids, weights, rows_by_y, per_row, after)


def local(
    tokens,
    out_grad,
    router_logits,
    routed_counts,
    routed_positions,
    gate_values,
    up_values,
    down_values,
    gate_scales,
    up_scales,
    down_scales,
):
    z, core, x = lax.axis_index("z"), lax.axis_index("core"), lax.axis_index("x")
    ids = jnp.stack([z, core, x]).astype(jnp.int32)

    scales = (gate_scales.T, up_scales.T, down_scales)
    held = own_tiles(ids, *scales, gate_values, up_values, down_values)
    held = jnp.concatenate([held] + [swap(held, "z", Z, mask) for mask in (4, 2, 6)], axis=0)
    mine = (held, swap(held, "z", Z, 1))
    theirs = tuple(swap(h, "core", CORES, 1) for h in mine)
    per_row = rates(router_logits.reshape(SEQ // T, T), routed_positions[None, :], routed_counts)

    own, p1, p2, p3, w_own = forward(ids, tokens, out_grad, mine, theirs)
    got = [swap(p, "x", XS, r) for r, p in ((1, p1), (2, p2), (3, p3))]
    total = reduce_rows(own, got)
    message = deltas(ids, total, swap(total, "zhi", Z_HI, 1), per_row)
    parts = [message] + [swap(message, "x", XS, r) for r in (1, 2, 3)]

    weights = lax.all_gather(w_own, "row")

    keep, send = weight_grads(ids, tokens, out_grad, per_row, parts)
    received = swap(send, "core", CORES, 1)
    arrived = swap(core_sum(keep, received), "z", Z, 1)

    rows_by_y = lax.all_gather(row_order(ids, parts, keep), "row")
    own_sum, s4, s2, s6 = pair_sum(keep, received, arrived)
    grad_tokens, grad_logits = token_grads(ids, weights, rows_by_y, per_row, s4)
    grad_gate, grad_up, grad_down = last_sum(
        own_sum,
        swap(s4, "z", Z, 4),
        swap(s2, "z", Z, 2),
        swap(s6, "z", Z, 6),
        grad_logits,
    )
    return (grad_tokens, grad_gate, grad_up, grad_down, grad_logits.reshape(SEQ))


def solution(mesh):
    fine = Mesh(mesh.devices.reshape(Z, CORES, ROWS, Z_HI, XS), AXES)
    dp, col = ("z", "core"), ("zhi", "x")
    placed = (
        P(dp, col),
        P(dp, col),
        P(dp),
        P(dp),
        P(dp),
        P(col + dp, "row"),
        P(col + dp, "row"),
        P("row", col + dp),
        P(col, "row"),
        P(col, "row"),
        P("row", col),
    )
    return jax.shard_map(
        local,
        mesh=fine,
        in_specs=placed,
        out_specs=(P(dp, col), P(col + dp, "row"), P(col + dp, "row"), P("row", col + dp), P(dp)),
        check_vma=False,
    )
```

```python
import jax
import jax.numpy as jnp
from jax import lax
from jax.experimental import pallas as pl
from jax.experimental.pallas import tpu as pltpu
from jax.sharding import Mesh, PartitionSpec as P

BF = jnp.bfloat16
F32 = jnp.float32
Z, CORES, ROWS, Z_HI, XS = 8, 2, 4, 2, 4
T = 128
CAP = 768
SEQ = 6144
D = 2048
RB = CAP // XS
MSG = RB + 16
AXES = ("z", "core", "row", "zhi", "x")
NT = (((1,), (1,)), ((), ()))


def swap(value, axis, size, mask):
    return lax.ppermute(value, axis, [(i, i ^ mask) for i in range(size)])


def far_first(i):
    return ((i & 1) << 2) | (i & 2) | ((i >> 2) & 1)


def split3(value):
    hi = value.astype(BF)
    rest = value - hi.astype(F32)
    mid = rest.astype(BF)
    return hi, mid, (rest - mid.astype(F32)).astype(BF)


def params(mib=44):
    return pltpu.CompilerParams(
        dimension_semantics=("arbitrary",), vmem_limit_bytes=mib * 1024 * 1024
    )


def work(flops, mib):
    return pl.CostEstimate(flops=flops, bytes_accessed=mib * 1024 * 1024, transcendentals=0)


VMEM = pl.BlockSpec(memory_space=pltpu.VMEM)
SMEM = pl.BlockSpec(memory_space=pltpu.SMEM)
ANY = pl.BlockSpec(memory_space=pl.ANY)
HBM = pl.BlockSpec(memory_space=pltpu.HBM)


def turn(row):
    return jnp.broadcast_to(row, (8, row.shape[1])).T[:, 0:1]


def rates_kernel(logits, positions, counts, out):
    place = turn(positions[...].astype(F32))
    at = place.astype(jnp.int32)
    lanes = lax.broadcasted_iota(jnp.int32, (CAP, T), 1)
    upper = jnp.where(lanes[:, 0 : SEQ // T] == (at >> 7), 1.0, 0.0).astype(BF)
    picked = jnp.zeros((CAP, T), F32)
    for piece in split3(logits[...]):
        picked = picked + jnp.dot(upper, piece, preferred_element_type=F32)
    logit = jnp.sum(jnp.where(lanes == (at & (T - 1)), picked, 0.0), axis=1, keepdims=True)
    rate = jax.nn.sigmoid(logit)
    row = lax.broadcasted_iota(jnp.int32, (CAP, 1), 0)
    live = jnp.where(row < counts[0], 1.0, 0.0)
    weight = rate * live
    slope = rate * (1.0 - rate) * live
    out[...] = jnp.where(lanes == 0, weight, jnp.where(lanes == 1, slope, place))


def rates(logits, positions, counts):
    return pl.pallas_call(
        rates_kernel,
        out_shape=jax.ShapeDtypeStruct((CAP, T), F32),
        in_specs=[VMEM, VMEM, SMEM],
        out_specs=VMEM,
        name="rates",
    )(logits, positions, counts)


def tile_kernel(ids, gs, us, ds, gate, up, down, out):
    dp = ids[0] * CORES + ids[1]
    lane = lax.broadcasted_iota(jnp.int32, (1, Z * CORES), 1)
    g, u, d = (
        jnp.sum(jnp.where(lane == dp, ref[...], 0.0), axis=1, keepdims=True) for ref in (gs, us, ds)
    )
    out[:, 0:T] = (gate[...].astype(F32) * g).astype(BF)
    out[:, T : 2 * T] = (up[...].astype(F32) * u).astype(BF)
    out[:, 2 * T : 3 * T] = (down[...].astype(F32) * d).T.astype(BF)


def own_tiles(ids, gate_scales, up_scales, down_scales, gate, up, down):
    return pl.pallas_call(
        tile_kernel,
        out_shape=jax.ShapeDtypeStruct((T, 3 * T), BF),
        in_specs=[SMEM] + [VMEM] * 6,
        out_specs=VMEM,
        name="own_tiles",
    )(ids, gate_scales, up_scales, down_scales, gate, up, down)


def forward_kernel(ids, tokens, out_grad, m0, m1, t0, t1, own, p1, p2, p3, w_out, w_down):
    step = pl.program_id(0)
    z, core = ids[0], ids[1]

    @pl.when(step == 0)
    def _():
        for i in range(Z):
            base = (z ^ far_first(i)) * (2 * T)
            for pair, side in (((m0, m1), core), ((t0, t1), 1 - core)):
                ref, j = pair[i // 4], i % 4
                rows = pl.ds(pl.multiple_of(base + side * T, T), T)
                w_out[rows, :] = ref[j * T : (j + 1) * T, 0 : 2 * T]
                w_down[rows, :] = ref[j * T : (j + 1) * T, 2 * T : 3 * T]

    gate_up = jnp.dot(tokens[...], w_out[...], preferred_element_type=F32)
    back = jnp.dot(out_grad[...], w_down[...], preferred_element_type=F32)

    @pl.when(step == 0)
    def _():
        own[:, 0 : 2 * T] = gate_up
        own[:, 2 * T : 3 * T] = back

    for k, ref in ((1, p1), (2, p2), (3, p3)):

        @pl.when(step == k)
        def _():
            ref[:, 0 : 2 * T] = gate_up.astype(BF)
            ref[:, 2 * T : 3 * T] = back.astype(BF)


def forward(ids, tokens, out_grad, mine, theirs):
    whole = lambda *shape: pl.BlockSpec(shape, lambda r, ids: (0,) * len(shape))
    rows = pl.BlockSpec((RB, D), lambda r, ids: (ids[2] ^ r, 0))
    part = jax.ShapeDtypeStruct((RB, 3 * T), BF)
    return pl.pallas_call(
        forward_kernel,
        grid_spec=pltpu.PrefetchScalarGridSpec(
            num_scalar_prefetch=1,
            grid=(XS,),
            in_specs=[rows, rows] + [whole(4 * T, 3 * T)] * 4,
            out_specs=[whole(RB, 3 * T)] * 4 + [whole(D, 2 * T)],
            scratch_shapes=[pltpu.VMEM((D, T), BF)],
        ),
        out_shape=[
            jax.ShapeDtypeStruct((RB, 3 * T), F32),
            part,
            part,
            part,
            jax.ShapeDtypeStruct((D, 2 * T), BF),
        ],
        compiler_params=params(),
        cost_estimate=work(2 * CAP * D * 3 * T, 10),
        name="forward",
    )(ids, tokens, out_grad, *mine, *theirs)


def delta_kernel(ids, s_mine, s_theirs, per_row, out):
    total = s_mine[...].astype(F32) + s_theirs[...].astype(F32)
    gate, up, back = total[:, 0:T], total[:, T : 2 * T], total[:, 2 * T : 3 * T]
    weight = per_row[pl.ds(pl.multiple_of(ids[2] * RB, RB), RB), :][:, 0:1]
    s = jax.nn.sigmoid(gate)
    act = gate * s
    hidden_full = act * up
    delta = back * weight
    out[0:RB, 0:T] = (delta * up * s * (1.0 + gate * (1.0 - s))).astype(BF)
    out[0:RB, T : 2 * T] = (delta * act).astype(BF)
    out[0:RB, 2 * T : 3 * T] = hidden_full.astype(BF)
    router = lax.dot_general(
        jnp.ones((8, T), F32),
        back * hidden_full,
        NT,
        precision=lax.Precision.HIGHEST,
        preferred_element_type=F32,
    )
    router = jnp.concatenate([router, jnp.zeros((8, 2 * T - RB), F32)], axis=1)
    hi, mid, low = (piece.astype(F32) for piece in split3(router))
    row = lax.broadcasted_iota(jnp.int32, (8, 2 * T), 0)
    pieces = jnp.where(row == 0, hi, jnp.where(row == 1, mid, jnp.where(row == 2, low, 0.0)))
    out[RB:MSG, 0 : 2 * T] = jnp.concatenate([pieces, jnp.zeros_like(pieces)], axis=0).astype(BF)
    out[RB:MSG, 2 * T : 3 * T] = jnp.zeros((16, T), BF)


def deltas(ids, s_mine, s_theirs, per_row):
    return pl.pallas_call(
        delta_kernel,
        out_shape=jax.ShapeDtypeStruct((MSG, 3 * T), BF),
        in_specs=[SMEM] + [VMEM] * 3,
        out_specs=VMEM,
        name="deltas",
    )(ids, s_mine, s_theirs, per_row)


def weight_grad_kernel(
    ids, tokens, out_grad, per_row, d0, d1, d2, d3, after, keep, send, rows_out, flat, turned
):
    step = pl.program_id(0)
    core, x = ids[1], ids[2]

    @pl.when(step == 0)
    def _():
        for r, ref in enumerate((d0, d1, d2, d3)):
            rows = pl.ds(pl.multiple_of((x ^ r) * RB, RB), RB)
            flat[rows, :] = ref[0:RB, :]
            rows_out[rows, :] = ref[0:RB, 0 : 2 * T]
            rows_out[CAP + 16 * r : CAP + 16 * (r + 1), :] = ref[RB:MSG, 0 : 2 * T]
        turned[...] = flat[...].astype(F32).T.astype(BF)

    scaled = (out_grad[...].astype(F32) * per_row[:, 0:1]).astype(BF)
    gate_up = jnp.dot(turned[0 : 2 * T, :], tokens[...], preferred_element_type=F32)
    down = jnp.dot(turned[2 * T : 3 * T, :], scaled, preferred_element_type=F32)
    for rows, value in ((slice(0, 2 * T), gate_up), (slice(2 * T, 3 * T), down)):
        low, high = value[:, 0:T].astype(BF), value[:, T : 2 * T].astype(BF)
        keep[rows, :] = jnp.where(core == 0, low, high)
        send[rows, :] = jnp.where(core == 0, high, low)


def weight_grads(ids, tokens, out_grad, per_row, parts, after):
    whole = lambda *shape: pl.BlockSpec(shape, lambda i, ids: (0,) * len(shape))
    columns = pl.BlockSpec((CAP, 2 * T), lambda i, ids: (0, ids[0] ^ far_first(i ^ 4)))
    block = pl.BlockSpec((3 * T, T), lambda i, ids: (i, 0))
    return pl.pallas_call(
        weight_grad_kernel,
        grid_spec=pltpu.PrefetchScalarGridSpec(
            num_scalar_prefetch=1,
            grid=(Z,),
            in_specs=[columns, columns, whole(CAP, T)] + [whole(MSG, 3 * T)] * 4 + [whole(16, T)],
            out_specs=[block, block, whole(CAP + XS * 16, 2 * T)],
            scratch_shapes=[pltpu.VMEM((CAP, 3 * T), BF), pltpu.VMEM((3 * T, CAP), BF)],
        ),
        out_shape=[
            jax.ShapeDtypeStruct((Z * 3 * T, T), BF),
            jax.ShapeDtypeStruct((Z * 3 * T, T), BF),
            jax.ShapeDtypeStruct((CAP + XS * 16, 2 * T), BF),
        ],
        compiler_params=params(),
        cost_estimate=work(2 * CAP * D * 3 * T, 10),
        name="weight_grads",
    )(ids, tokens, out_grad, per_row, *parts, after)


def last_sum_kernel(own, r4, r2, r6, after, gate, up, down):
    total = own[...] + r4[...].astype(F32) + r2[...].astype(F32) + r6[...].astype(F32)
    gate[...] = total[0:T].T
    up[...] = total[T : 2 * T].T
    down[...] = total[2 * T : 3 * T]


def last_sum(own, r4, r2, r6, after):
    return pl.pallas_call(
        last_sum_kernel,
        out_shape=[jax.ShapeDtypeStruct((T, T), F32)] * 3,
        in_specs=[VMEM] * 4 + [ANY],
        out_specs=[VMEM] * 3,
        name="last_sum",
    )(own, r4, r2, r6, after)


def token_grad_kernel(
    ids, weights, rows_by_y, per_row, after, out, logits_out, router
):
    step = pl.program_id(0)
    x = ids[2]

    @pl.when(step == 0)
    def _():
        for r in range(XS):
            rows = slice(CAP + 16 * r, CAP + 16 * (r + 1))
            terms = []
            for j in range(ROWS):
                pieces = rows_by_y[j, rows, :].astype(F32)
                terms.append(pieces[0:1] + pieces[1:2] + pieces[2:3])
            total = (terms[0] + terms[1]) + (terms[2] + terms[3])
            router[pl.ds(pl.multiple_of((x ^ r) * RB, RB), RB), :] = turn(total)[0:RB]
        value = router[...] * per_row[:, 1:2]
        at = per_row[:, 2:3].astype(jnp.int32)
        lanes = lax.broadcasted_iota(jnp.int32, (CAP, T), 1)
        upper = jnp.where(lanes == (at >> 7), 1.0, 0.0).T.astype(BF)
        spread = jnp.where(lanes == (at & (T - 1)), value, 0.0)
        total = jnp.zeros((T, T), F32)
        for piece in split3(spread):
            total = total + jnp.dot(upper, piece, preferred_element_type=F32)
        logits_out[...] = total[0 : SEQ // T, :]

    total = jnp.zeros((CAP, 2 * T), F32)
    for j in range(ROWS):
        total += lax.dot_general(
            rows_by_y[j, 0:CAP, :], weights[j], NT, preferred_element_type=F32
        )
    out[...] = total.astype(BF)


def token_grads(ids, weights, rows_by_y, per_row, after):
    whole = lambda *shape: pl.BlockSpec(shape, lambda i, ids: (0,) * len(shape))
    return pl.pallas_call(
        token_grad_kernel,
        grid_spec=pltpu.PrefetchScalarGridSpec(
            num_scalar_prefetch=1,
            grid=(Z,),
            in_specs=[
                pl.BlockSpec((ROWS, 2 * T, 2 * T), lambda i, ids: (0, i, 0)),
                whole(ROWS, CAP + XS * 16, 2 * T),
                whole(CAP, T),
                ANY,
            ],
            out_specs=[
                pl.BlockSpec((CAP, 2 * T), lambda i, ids: (0, i)),
                whole(SEQ // T, T),
            ],
            scratch_shapes=[pltpu.VMEM((CAP, 1), F32)],
        ),
        out_shape=[
            jax.ShapeDtypeStruct((CAP, D), BF),
            jax.ShapeDtypeStruct((SEQ // T, T), F32),
        ],
        compiler_params=params(),
        cost_estimate=work(2 * CAP * D * 8 * T, 12),
        name="token_grads",
    )(ids, weights, rows_by_y, per_row, after)


def local(
    tokens,
    out_grad,
    router_logits,
    routed_counts,
    routed_positions,
    gate_values,
    up_values,
    down_values,
    gate_scales,
    up_scales,
    down_scales,
):
    z, core, x = lax.axis_index("z"), lax.axis_index("core"), lax.axis_index("x")
    ids = jnp.stack([z, core, x]).astype(jnp.int32)

    scales = (gate_scales.T, up_scales.T, down_scales)
    held = own_tiles(ids, *scales, gate_values, up_values, down_values)
    held = jnp.concatenate([held] + [swap(held, "z", Z, mask) for mask in (4, 2, 6)], axis=0)
    mine = (held, swap(held, "z", Z, 1))
    theirs = tuple(swap(h, "core", CORES, 1) for h in mine)
    per_row = rates(router_logits.reshape(SEQ // T, T), routed_positions[None, :], routed_counts)

    own, p1, p2, p3, w_own = forward(ids, tokens, out_grad, mine, theirs)
    got = [swap(p, "x", XS, r) for r, p in ((1, p1), (2, p2), (3, p3))]
    total = own
    for g in got:
        total = total + g.astype(F32)
    total = total.astype(BF)
    message = deltas(ids, total, swap(total, "zhi", Z_HI, 1), per_row)
    parts = [message] + [swap(message, "x", XS, r) for r in (1, 2, 3)]

    weights = lax.all_gather(w_own, "row")

    keep, send, rows = weight_grads(
        ids, tokens, out_grad, per_row, parts, weights[0, 0:16, 0:T]
    )
    sums = keep.astype(F32) + swap(send, "core", CORES, 1).astype(F32)
    near, rest = sums[0 : 4 * 3 * T].astype(BF), sums[4 * 3 * T :]
    sums = rest + swap(near, "z", Z, 1).astype(F32)
    own_sum, *others = (sums[i * 3 * T : (i + 1) * 3 * T] for i in range(4))
    s4, s2, s6 = (other.astype(BF) for other in others)

    rows_by_y = lax.all_gather(rows, "row")
    grad_tokens, grad_logits = token_grads(ids, weights, rows_by_y, per_row, s4)
    grad_gate, grad_up, grad_down = last_sum(
        own_sum,
        swap(s4, "z", Z, 4),
        swap(s2, "z", Z, 2),
        swap(s6, "z", Z, 6),
        grad_logits,
    )
    return (grad_tokens, grad_gate, grad_up, grad_down, grad_logits.reshape(SEQ))


def solution(mesh):
    fine = Mesh(mesh.devices.reshape(Z, CORES, ROWS, Z_HI, XS), AXES)
    dp, col = ("z", "core"), ("zhi", "x")
    placed = (
        P(dp, col),
        P(dp, col),
        P(dp),
        P(dp),
        P(dp),
        P(col + dp, "row"),
        P(col + dp, "row"),
        P("row", col + dp),
        P(col, "row"),
        P(col, "row"),
        P("row", col),
    )
    return jax.shard_map(
        local,
        mesh=fine,
        in_specs=placed,
        out_specs=(P(dp, col), P(col + dp, "row"), P(col + dp, "row"), P("row", col + dp), P(dp)),
        check_vma=False,
    )
```

```python
import jax
import jax.numpy as jnp
from jax import lax
from jax.experimental import pallas as pl
from jax.experimental.pallas import tpu as pltpu
from jax.sharding import Mesh, PartitionSpec as P

BF = jnp.bfloat16
F32 = jnp.float32
Z, CORES, ROWS, Z_HI, XS = 8, 2, 4, 2, 4
T = 128
CAP = 768
SEQ = 6144
D = 2048
RB = CAP // XS
PAD = 192
MSG = RB + 16
AXES = ("z", "core", "row", "zhi", "x")
NT = (((1,), (1,)), ((), ()))


def swap(value, axis, size, mask):
    return lax.ppermute(value, axis, [(i, i ^ mask) for i in range(size)])


def far_first(i):
    return ((i & 1) << 2) | (i & 2) | ((i >> 2) & 1)


def split3(value):
    hi = value.astype(BF)
    rest = value - hi.astype(F32)
    mid = rest.astype(BF)
    return hi, mid, (rest - mid.astype(F32)).astype(BF)


def params(mib=20):
    return pltpu.CompilerParams(vmem_limit_bytes=mib * 1024 * 1024)


def work(flops, mib):
    return pl.CostEstimate(flops=flops, bytes_accessed=mib * 1024 * 1024, transcendentals=0)


VMEM = pl.BlockSpec(memory_space=pltpu.VMEM)
SMEM = pl.BlockSpec(memory_space=pltpu.SMEM)
ANY = pl.BlockSpec(memory_space=pl.ANY)
HBM = pl.BlockSpec(memory_space=pltpu.HBM)


def in_hbm(*arrays):
    return tuple(pltpu.with_memory_space_constraint(array, pltpu.HBM) for array in arrays)


def turn(row):
    return jnp.broadcast_to(row, (8, row.shape[1])).T[:, 0:1]


def rates_kernel(logits, positions, counts, out):
    place = turn(positions[...].astype(F32))
    at = place.astype(jnp.int32)
    lanes = lax.broadcasted_iota(jnp.int32, (CAP, T), 1)
    upper = jnp.where(lanes[:, 0 : SEQ // T] == (at >> 7), 1.0, 0.0).astype(BF)
    picked = jnp.zeros((CAP, T), F32)
    for piece in split3(logits[...]):
        picked = picked + jnp.dot(upper, piece, preferred_element_type=F32)
    logit = jnp.sum(jnp.where(lanes == (at & (T - 1)), picked, 0.0), axis=1, keepdims=True)
    rate = jax.nn.sigmoid(logit)
    row = lax.broadcasted_iota(jnp.int32, (CAP, 1), 0)
    live = jnp.where(row < counts[0], 1.0, 0.0)
    weight = rate * live
    slope = rate * (1.0 - rate) * live
    out[...] = jnp.where(lanes == 0, weight, jnp.where(lanes == 1, slope, place))


def rates(logits, positions, counts):
    return pl.pallas_call(
        rates_kernel,
        out_shape=jax.ShapeDtypeStruct((CAP, T), F32),
        in_specs=[VMEM, VMEM, SMEM],
        out_specs=VMEM,
        compiler_params=params(8),
        name="rates",
    )(logits, positions, counts)


def tile_kernel(ids, gs, us, ds, gate, up, down, out):
    dp = ids[0] * CORES + ids[1]
    lane = lax.broadcasted_iota(jnp.int32, (1, Z * CORES), 1)
    g, u, d = (
        jnp.sum(jnp.where(lane == dp, ref[...], 0.0), axis=1, keepdims=True) for ref in (gs, us, ds)
    )
    out[:, 0:T] = (gate[...].astype(F32) * g).astype(BF)
    out[:, T : 2 * T] = (up[...].astype(F32) * u).astype(BF)
    out[:, 2 * T : 3 * T] = (down[...].astype(F32) * d).T.astype(BF)


def own_tiles(ids, gate_scales, up_scales, down_scales, gate, up, down):
    return pl.pallas_call(
        tile_kernel,
        out_shape=jax.ShapeDtypeStruct((T, 3 * T), BF),
        in_specs=[SMEM] + [VMEM] * 6,
        out_specs=VMEM,
        compiler_params=params(8),
        name="own_tiles",
    )(ids, *in_hbm(gate_scales, up_scales, down_scales, gate, up, down))


def load_kernel(tokens, out_grad, tokens_out, out_grad_out, sems):
    copies = (
        pltpu.make_async_copy(tokens, tokens_out, sems.at[0]),
        pltpu.make_async_copy(out_grad, out_grad_out, sems.at[1]),
    )
    for copy in copies:
        copy.start()
    for copy in copies:
        copy.wait()


def load(tokens, out_grad):
    return pl.pallas_call(
        load_kernel,
        out_shape=[pltpu.VMEM((CAP, D), BF)] * 2,
        in_specs=[ANY] * 2,
        out_specs=[ANY] * 2,
        scratch_shapes=[pltpu.SemaphoreType.DMA((2,))],
        compiler_params=params(1),
        name="load",
    )(*in_hbm(tokens, out_grad))


def join_kernel(a, b, c, d, tokens, out_grad, out):
    for i, ref in enumerate((a, b, c, d)):
        out[i * T : (i + 1) * T, :] = ref[...]


def join(blocks, tokens, out_grad):
    return pl.pallas_call(
        join_kernel,
        out_shape=jax.ShapeDtypeStruct((4 * T, 3 * T), BF),
        in_specs=[VMEM] * 4 + [ANY] * 2,
        out_specs=VMEM,
        compiler_params=params(8),
        name="join",
    )(*blocks, tokens, out_grad)


def forward_kernel(ids, tokens, out_grad, m0, m1, t0, t1, own, p1, p2, p3, w_both, w_down):
    step = pl.program_id(0)
    z, core = ids[0], ids[1]

    @pl.when(step == 0)
    def _():
        for i in range(Z):
            base = (z ^ far_first(i)) * (2 * T)
            for pair, side in (((m0, m1), core), ((t0, t1), 1 - core)):
                ref, j = pair[i // 4], i % 4
                rows = pl.ds(pl.multiple_of(base + side * T, T), T)
                w_both[rows, :] = ref[j * T : (j + 1) * T, 0 : 2 * T]
                w_down[rows, :] = ref[j * T : (j + 1) * T, 2 * T : 3 * T]

    gate_up = jnp.dot(tokens[...], w_both[...], preferred_element_type=F32)
    back = jnp.dot(out_grad[...], w_down[...], preferred_element_type=F32)

    @pl.when(step == 0)
    def _():
        own[:, 0 : 2 * T] = gate_up
        own[:, 2 * T : 3 * T] = back

    for k, ref in ((1, p1), (2, p2), (3, p3)):

        @pl.when(step == k)
        def _():
            ref[:, 0 : 2 * T] = gate_up.astype(BF)
            ref[:, 2 * T : 3 * T] = back.astype(BF)


def forward(ids, tokens, out_grad, mine, theirs):
    whole = lambda *shape: pl.BlockSpec(shape, lambda r, ids: (0,) * len(shape))
    rows = pl.BlockSpec((RB, D), lambda r, ids: (ids[2] ^ r, 0))
    part = pltpu.HBM((RB, 3 * T), BF)
    return pl.pallas_call(
        forward_kernel,
        grid_spec=pltpu.PrefetchScalarGridSpec(
            num_scalar_prefetch=1,
            grid=(XS,),
            in_specs=[rows, rows] + [whole(4 * T, 3 * T)] * 4,
            out_specs=[whole(RB, 3 * T)] * 4 + [whole(D, 2 * T)],
            scratch_shapes=[pltpu.VMEM((D, T), BF)],
        ),
        out_shape=[
            jax.ShapeDtypeStruct((RB, 3 * T), F32),
            part,
            part,
            part,
            pltpu.HBM((D, 2 * T), BF),
        ],
        compiler_params=params(),
        cost_estimate=work(2 * CAP * D * 3 * T, 10),
        name="forward",
    )(ids, tokens, out_grad, *mine, *theirs)


def delta_kernel(ids, s_mine, s_theirs, per_row, out):
    total = s_mine[...].astype(F32) + s_theirs[...].astype(F32)
    gate, up, back = total[:, 0:T], total[:, T : 2 * T], total[:, 2 * T : 3 * T]
    weight = per_row[pl.ds(pl.multiple_of(ids[2] * RB, RB), RB), :][:, 0:1]
    s = jax.nn.sigmoid(gate)
    act = gate * s
    hidden_full = act * up
    delta = back * weight
    out[0:RB, 0:T] = (delta * up * s * (1.0 + gate * (1.0 - s))).astype(BF)
    out[0:RB, T : 2 * T] = (delta * act).astype(BF)
    out[0:RB, 2 * T : 3 * T] = hidden_full.astype(BF)
    router = lax.dot_general(
        jnp.ones((8, T), F32),
        back * hidden_full,
        NT,
        precision=lax.Precision.HIGHEST,
        preferred_element_type=F32,
    )
    router = jnp.concatenate([router, jnp.zeros((8, 2 * T - RB), F32)], axis=1)
    hi, mid, low = (piece.astype(F32) for piece in split3(router))
    row = lax.broadcasted_iota(jnp.int32, (8, 2 * T), 0)
    pieces = jnp.where(row == 0, hi, jnp.where(row == 1, mid, jnp.where(row == 2, low, 0.0)))
    out[RB:MSG, 0 : 2 * T] = jnp.concatenate([pieces, jnp.zeros_like(pieces)], axis=0).astype(BF)
    out[RB:MSG, 2 * T : 3 * T] = jnp.zeros((16, T), BF)


def deltas(ids, s_mine, s_theirs, per_row):
    return pl.pallas_call(
        delta_kernel,
        out_shape=jax.ShapeDtypeStruct((MSG, 3 * T), BF),
        in_specs=[SMEM] + [VMEM] * 3,
        out_specs=VMEM,
        compiler_params=params(8),
        name="deltas",
    )(ids, s_mine, s_theirs, per_row)


def weight_grad_kernel(
    ids, tokens, out_grad, per_row, d0, d1, d2, d3, keep, send, flat, turned
):
    step = pl.program_id(0)
    core, x = ids[1], ids[2]

    @pl.when(step == 0)
    def _():
        for r, ref in enumerate((d0, d1, d2, d3)):
            rows = pl.ds(pl.multiple_of((x ^ r) * RB, RB), RB)
            flat[rows, :] = ref[0:RB, :]
        turned[...] = flat[...].astype(F32).T.astype(BF)

    scaled = (out_grad[...].astype(F32) * per_row[:, 0:1]).astype(BF)
    gate_up = jnp.dot(turned[0 : 2 * T, :], tokens[...], preferred_element_type=F32)
    down = jnp.dot(turned[2 * T : 3 * T, :], scaled, preferred_element_type=F32)
    for rows, value in ((slice(0, 2 * T), gate_up), (slice(2 * T, 3 * T), down)):
        low, high = value[:, 0:T].astype(BF), value[:, T : 2 * T].astype(BF)
        keep[rows, :] = jnp.where(core == 0, low, high)
        send[rows, :] = jnp.where(core == 0, high, low)


def weight_grads(ids, tokens, out_grad, per_row, parts):
    whole = lambda *shape: pl.BlockSpec(shape, lambda i, ids: (0,) * len(shape))
    columns = pl.BlockSpec((CAP, 2 * T), lambda i, ids: (0, ids[0] ^ far_first(i ^ 4)))
    block = pl.BlockSpec((3 * T, T), lambda i, ids: (i, 0))
    return pl.pallas_call(
        weight_grad_kernel,
        grid_spec=pltpu.PrefetchScalarGridSpec(
            num_scalar_prefetch=1,
            grid=(Z,),
            in_specs=[columns, columns, whole(CAP, T)] + [whole(MSG, 3 * T)] * 4,
            out_specs=[block, block],
            scratch_shapes=[pltpu.VMEM((CAP, 3 * T), BF), pltpu.VMEM((3 * T, CAP), BF)],
        ),
        out_shape=[
            jax.ShapeDtypeStruct((Z * 3 * T, T), BF),
            jax.ShapeDtypeStruct((Z * 3 * T, T), BF),
        ],
        compiler_params=params(),
        cost_estimate=work(2 * CAP * D * 3 * T, 10),
        name="weight_grads",
    )(ids, tokens, out_grad, per_row, *parts)


def rows_kernel(ids, d0, d1, d2, d3, after, out):
    x = ids[2]
    for r, ref in enumerate((d0, d1, d2, d3)):
        rows = pl.ds(pl.multiple_of((x ^ r) * RB, RB), RB)
        out[rows, :] = ref[0:RB, 0 : 2 * T]
        out[CAP + 16 * r : CAP + 16 * (r + 1), :] = ref[RB:MSG, 0 : 2 * T]


def row_order(ids, parts, after):
    return pl.pallas_call(
        rows_kernel,
        out_shape=jax.ShapeDtypeStruct((CAP + XS * 16, 2 * T), BF),
        in_specs=[SMEM] + [VMEM] * 4 + [ANY],
        out_specs=VMEM,
        compiler_params=params(8),
        name="row_order",
    )(ids, *parts, after)


def core_sum_kernel(keep, received, send):
    rows = slice(0, 4 * 3 * T)
    send[rows, :] = (keep[rows, :].astype(F32) + received[rows, :].astype(F32)).astype(BF)
    send[4 * 3 * T :, :] = jnp.zeros((PAD, T), BF)


def core_sum(keep, received):
    return pl.pallas_call(
        core_sum_kernel,
        out_shape=jax.ShapeDtypeStruct((4 * 3 * T + PAD, T), BF),
        in_specs=[VMEM] * 2,
        out_specs=VMEM,
        compiler_params=params(8),
        name="core_sum",
    )(keep, received)


def pair_sum_kernel(keep, received, arrived, own, s4, s2, s6):
    for i, out in enumerate((own, s4, s2, s6)):
        there = slice(i * 3 * T, (i + 1) * 3 * T)
        here = slice((i + 4) * 3 * T, (i + 5) * 3 * T)
        total = keep[here, :].astype(F32) + received[here, :].astype(F32)
        out[...] = (total + arrived[there, :].astype(F32)).astype(out.dtype)


def pair_sum(keep, received, arrived):
    part = jax.ShapeDtypeStruct((3 * T, T), BF)
    return pl.pallas_call(
        pair_sum_kernel,
        out_shape=[jax.ShapeDtypeStruct((3 * T, T), F32), part, part, part],
        in_specs=[VMEM] * 3,
        out_specs=[VMEM] * 4,
        compiler_params=params(8),
        name="pair_sum",
    )(keep, received, arrived)


def last_sum_kernel(own, r4, r2, r6, after, gate, up, down):
    total = own[...] + r4[...].astype(F32) + r2[...].astype(F32) + r6[...].astype(F32)
    gate[...] = total[0:T].T
    up[...] = total[T : 2 * T].T
    down[...] = total[2 * T : 3 * T]


def last_sum(own, r4, r2, r6, after):
    return pl.pallas_call(
        last_sum_kernel,
        out_shape=[jax.ShapeDtypeStruct((T, T), F32)] * 3,
        in_specs=[VMEM] * 4 + [ANY],
        out_specs=[VMEM] * 3,
        compiler_params=params(8),
        name="last_sum",
    )(own, r4, r2, r6, *in_hbm(after))


def token_grad_kernel(
    ids, weights, y0, y1, y2, y3, per_row, after, out, logits_out, router, flat, w
):
    step = pl.program_id(0)
    x, y = ids[2], ids[3]
    rows_by_y = (y0, y1, y2, y3)

    @pl.when(step == 0)
    def _():
        for j in range(ROWS):
            flat[:, j * 2 * T : (j + 1) * 2 * T] = rows_by_y[j][0:CAP, :]
        for r in range(XS):
            place = pl.ds(pl.multiple_of((x ^ r) * RB, RB), RB)
            terms = []
            for j in range(ROWS):
                pieces = rows_by_y[j][CAP + 16 * r : CAP + 16 * (r + 1), :].astype(F32)
                terms.append(pieces[0:1] + pieces[1:2] + pieces[2:3])
            total = (terms[0] + terms[1]) + (terms[2] + terms[3])
            router[place, :] = turn(total)[0:RB]
        value = router[...] * per_row[:, 1:2]
        at = per_row[:, 2:3].astype(jnp.int32)
        lanes = lax.broadcasted_iota(jnp.int32, (CAP, T), 1)
        upper = jnp.where(lanes == (at >> 7), 1.0, 0.0).T.astype(BF)
        spread = jnp.where(lanes == (at & (T - 1)), value, 0.0)
        total = jnp.zeros((T, T), F32)
        for piece in split3(spread):
            total = total + jnp.dot(upper, piece, preferred_element_type=F32)
        logits_out[...] = total[0 : SEQ // T, :]

    for j in range(ROWS):
        w[:, j * 2 * T : (j + 1) * 2 * T] = weights[y ^ j]
    out[...] = lax.dot_general(flat[...], w[...], NT, preferred_element_type=F32).astype(BF)


def token_grads(ids, weights, rows_by_y, per_row, after):
    whole = lambda *shape: pl.BlockSpec(shape, lambda i, ids: (0,) * len(shape))
    return pl.pallas_call(
        token_grad_kernel,
        grid_spec=pltpu.PrefetchScalarGridSpec(
            num_scalar_prefetch=1,
            grid=(Z,),
            in_specs=[
                pl.BlockSpec((ROWS, 2 * T, 2 * T), lambda i, ids: (0, i, 0)),
            ]
            + [whole(CAP + XS * 16, 2 * T)] * 4
            + [whole(CAP, T), ANY],
            out_specs=[
                pl.BlockSpec((CAP, 2 * T), lambda i, ids: (0, i)),
                whole(SEQ // T, T),
            ],
            scratch_shapes=[
                pltpu.VMEM((CAP, 1), F32),
                pltpu.VMEM((CAP, 8 * T), BF),
                pltpu.VMEM((2 * T, 8 * T), BF),
            ],
        ),
        out_shape=[
            jax.ShapeDtypeStruct((CAP, D), BF),
            jax.ShapeDtypeStruct((SEQ // T, T), F32),
        ],
        compiler_params=params(),
        cost_estimate=work(2 * CAP * D * 8 * T, 12),
        name="token_grads",
    )(ids, weights, *rows_by_y, per_row, after)


def local(
    tokens,
    out_grad,
    router_logits,
    routed_counts,
    routed_positions,
    gate_values,
    up_values,
    down_values,
    gate_scales,
    up_scales,
    down_scales,
):
    ids = jnp.stack([lax.axis_index(axis) for axis in ("z", "core", "x", "row")]).astype(jnp.int32)

    scales = (gate_scales.T, up_scales.T, down_scales)
    held = own_tiles(ids, *scales, gate_values, up_values, down_values)
    tokens, out_grad = load(tokens, out_grad)
    held = join([held] + [swap(held, "z", Z, mask) for mask in (4, 2, 6)], tokens, out_grad)
    mine = (held, swap(held, "z", Z, 1))
    theirs = tuple(swap(h, "core", CORES, 1) for h in mine)
    per_row = rates(router_logits.reshape(SEQ // T, T), routed_positions[None, :], routed_counts)

    own, p1, p2, p3, w_own = forward(ids, tokens, out_grad, mine, theirs)
    got = [swap(p, "x", XS, r) for r, p in ((1, p1), (2, p2), (3, p3))]
    total = own
    for g in got:
        total = total + g.astype(F32)
    total = total.astype(BF)
    message = deltas(ids, total, swap(total, "zhi", Z_HI, 1), per_row)
    parts = [message] + [swap(message, "x", XS, r) for r in (1, 2, 3)]

    weights = lax.all_gather(w_own, "row")

    keep, send = weight_grads(ids, tokens, out_grad, per_row, parts)
    received = swap(send, "core", CORES, 1)
    sent = core_sum(keep, received)
    arrived = swap(sent, "z", Z, 1)

    rows = row_order(ids, parts, sent)
    y1, y2, y3 = (swap(rows, "row", ROWS, r) for r in (1, 2, 3))
    own_sum, s4, s2, s6 = pair_sum(keep, received, arrived)
    grad_tokens, grad_logits = token_grads(
        ids, weights, (rows, y1, y2, y3), per_row, s4
    )
    grad_gate, grad_up, grad_down = last_sum(
        own_sum,
        swap(s4, "z", Z, 4),
        swap(s2, "z", Z, 2),
        swap(s6, "z", Z, 6),
        grad_logits,
    )
    return (grad_tokens, grad_gate, grad_up, grad_down, grad_logits.reshape(SEQ))


def solution(mesh):
    fine = Mesh(mesh.devices.reshape(Z, CORES, ROWS, Z_HI, XS), AXES)
    dp, col = ("z", "core"), ("zhi", "x")
    placed = (
        P(dp, col),
        P(dp, col),
        P(dp),
        P(dp),
        P(dp),
        P(col + dp, "row"),
        P(col + dp, "row"),
        P("row", col + dp),
        P(col, "row"),
        P(col, "row"),
        P("row", col),
    )
    return jax.shard_map(
        local,
        mesh=fine,
        in_specs=placed,
        out_specs=(P(dp, col), P(col + dp, "row"), P(col + dp, "row"), P("row", col + dp), P(dp)),
        check_vma=False,
    )
```

```python
import jax
import jax.numpy as jnp
from jax import lax
from jax.experimental import pallas as pl
from jax.experimental.pallas import tpu as pltpu
from jax.sharding import Mesh, PartitionSpec as P

BF = jnp.bfloat16
F32 = jnp.float32
Z, CORES, ROWS, Z_HI, XS = 8, 2, 4, 2, 4
T = 128
CAP = 768
SEQ = 6144
D = 2048
RB = CAP // XS
PAD = 192
WIDE = 512
MSG = RB + 16
AXES = ("z", "core", "row", "zhi", "x")
NT = (((1,), (1,)), ((), ()))


def swap(value, axis, size, mask):
    return lax.ppermute(value, axis, [(i, i ^ mask) for i in range(size)])


def far_first(i):
    return ((i & 1) << 2) | (i & 2) | ((i >> 2) & 1)


def split3(value):
    hi = value.astype(BF)
    rest = value - hi.astype(F32)
    mid = rest.astype(BF)
    return hi, mid, (rest - mid.astype(F32)).astype(BF)


def params(mib=20):
    return pltpu.CompilerParams(vmem_limit_bytes=mib * 1024 * 1024)


def work(flops, mib):
    return pl.CostEstimate(flops=flops, bytes_accessed=mib * 1024 * 1024, transcendentals=0)


VMEM = pl.BlockSpec(memory_space=pltpu.VMEM)
SMEM = pl.BlockSpec(memory_space=pltpu.SMEM)
ANY = pl.BlockSpec(memory_space=pl.ANY)
HBM = pl.BlockSpec(memory_space=pltpu.HBM)


def in_hbm(*arrays):
    return tuple(pltpu.with_memory_space_constraint(array, pltpu.HBM) for array in arrays)


def turn(row):
    return jnp.broadcast_to(row, (8, row.shape[1])).T[:, 0:1]


def rates_kernel(logits, positions, counts, out):
    place = turn(positions[...].astype(F32))
    at = place.astype(jnp.int32)
    lanes = lax.broadcasted_iota(jnp.int32, (CAP, T), 1)
    upper = jnp.where(lanes[:, 0 : SEQ // T] == (at >> 7), 1.0, 0.0).astype(BF)
    picked = jnp.zeros((CAP, T), F32)
    for piece in split3(logits[...]):
        picked = picked + jnp.dot(upper, piece, preferred_element_type=F32)
    logit = jnp.sum(jnp.where(lanes == (at & (T - 1)), picked, 0.0), axis=1, keepdims=True)
    rate = jax.nn.sigmoid(logit)
    row = lax.broadcasted_iota(jnp.int32, (CAP, 1), 0)
    live = jnp.where(row < counts[0], 1.0, 0.0)
    weight = rate * live
    slope = rate * (1.0 - rate) * live
    out[...] = jnp.where(lanes == 0, weight, jnp.where(lanes == 1, slope, place))


def rates(logits, positions, counts):
    return pl.pallas_call(
        rates_kernel,
        out_shape=jax.ShapeDtypeStruct((CAP, T), F32),
        in_specs=[VMEM, VMEM, SMEM],
        out_specs=VMEM,
        compiler_params=params(8),
        name="rates",
    )(logits, positions, counts)


def tile_kernel(ids, gs, us, ds, gate, up, down, out):
    dp = ids[0] * CORES + ids[1]
    lane = lax.broadcasted_iota(jnp.int32, (1, Z * CORES), 1)
    g, u, d = (
        jnp.sum(jnp.where(lane == dp, ref[...], 0.0), axis=1, keepdims=True) for ref in (gs, us, ds)
    )
    out[:, 0:T] = (gate[...].astype(F32) * g).astype(BF)
    out[:, T : 2 * T] = (up[...].astype(F32) * u).astype(BF)
    out[:, 2 * T : 3 * T] = (down[...].astype(F32) * d).T.astype(BF)


def own_tiles(ids, gate_scales, up_scales, down_scales, gate, up, down):
    return pl.pallas_call(
        tile_kernel,
        out_shape=jax.ShapeDtypeStruct((T, 3 * T), BF),
        in_specs=[SMEM] + [VMEM] * 6,
        out_specs=VMEM,
        compiler_params=params(8),
        name="own_tiles",
    )(ids, *in_hbm(gate_scales, up_scales, down_scales, gate, up, down))


def load_kernel(*refs):
    n = len(refs) // 2
    copies = [pltpu.make_async_copy(refs[i], refs[n + i], refs[-1].at[i]) for i in range(n)]
    for copy in copies:
        copy.start()
    for copy in copies:
        copy.wait()


def load(*arrays):
    n = len(arrays)
    return pl.pallas_call(
        load_kernel,
        out_shape=[pltpu.VMEM(array.shape, array.dtype) for array in arrays],
        in_specs=[ANY] * n,
        out_specs=[ANY] * n,
        scratch_shapes=[pltpu.SemaphoreType.DMA((n,))],
        compiler_params=params(1),
        name="load",
    )(*in_hbm(*arrays))


def join_kernel(a, b, c, d, tokens, out_grad, out):
    for i, ref in enumerate((a, b, c, d)):
        out[i * T : (i + 1) * T, :] = ref[...]


def join(blocks, tokens, out_grad):
    return pl.pallas_call(
        join_kernel,
        out_shape=jax.ShapeDtypeStruct((4 * T, 3 * T), BF),
        in_specs=[VMEM] * 4 + [ANY] * 2,
        out_specs=VMEM,
        compiler_params=params(8),
        name="join",
    )(*blocks, tokens, out_grad)


def forward_kernel(ids, tokens, out_grad, m0, m1, t0, t1, own, p1, p2, p3, w_out, w_both, w_down, sem):
    step = pl.program_id(0)
    z, core = ids[0], ids[1]

    @pl.when(step == 0)
    def _():
        for i in range(Z):
            base = (z ^ far_first(i)) * (2 * T)
            for pair, side in (((m0, m1), core), ((t0, t1), 1 - core)):
                ref, j = pair[i // 4], i % 4
                rows = pl.ds(pl.multiple_of(base + side * T, T), T)
                w_both[rows, :] = ref[j * T : (j + 1) * T, 0 : 2 * T]
                w_down[rows, :] = ref[j * T : (j + 1) * T, 2 * T : 3 * T]

        pltpu.make_async_copy(w_both, w_out, sem).start()

    gate_up = jnp.dot(tokens[...], w_both[...], preferred_element_type=F32)
    back = jnp.dot(out_grad[...], w_down[...], preferred_element_type=F32)

    @pl.when(step == 0)
    def _():
        own[:, 0 : 2 * T] = gate_up
        own[:, 2 * T : 3 * T] = back

    for k, ref in ((1, p1), (2, p2), (3, p3)):

        @pl.when(step == k)
        def _():
            ref[:, 0 : 2 * T] = gate_up.astype(BF)
            ref[:, 2 * T : 3 * T] = back.astype(BF)

    @pl.when(step == XS - 1)
    def _():
        pltpu.make_async_copy(w_both, w_out, sem).wait()


def forward(ids, tokens, out_grad, mine, theirs):
    whole = lambda *shape: pl.BlockSpec(shape, lambda r, ids: (0,) * len(shape))
    rows = pl.BlockSpec((RB, D), lambda r, ids: (ids[2] ^ r, 0))
    part = pltpu.HBM((RB, 3 * T), BF)
    return pl.pallas_call(
        forward_kernel,
        grid_spec=pltpu.PrefetchScalarGridSpec(
            num_scalar_prefetch=1,
            grid=(XS,),
            in_specs=[rows, rows] + [whole(4 * T, 3 * T)] * 4,
            out_specs=[whole(RB, 3 * T)] * 4 + [ANY],
            scratch_shapes=[
                pltpu.VMEM((D, 2 * T), BF),
                pltpu.VMEM((D, T), BF),
                pltpu.SemaphoreType.DMA,
            ],
        ),
        out_shape=[
            jax.ShapeDtypeStruct((RB, 3 * T), F32),
            part,
            part,
            part,
            pltpu.HBM((D, 2 * T), BF),
        ],
        compiler_params=params(),
        cost_estimate=work(2 * CAP * D * 3 * T, 10),
        name="forward",
    )(ids, tokens, out_grad, *mine, *theirs)


def reduce_kernel(own, g1, g2, g3, total):
    total[...] = (
        own[...] + g1[...].astype(F32) + g2[...].astype(F32) + g3[...].astype(F32)
    ).astype(BF)


def reduce_rows(own, got):
    return pl.pallas_call(
        reduce_kernel,
        out_shape=jax.ShapeDtypeStruct((RB, 3 * T), BF),
        in_specs=[VMEM] * 4,
        out_specs=VMEM,
        compiler_params=params(8),
        cost_estimate=work(20_000_000_000, 2),
        name="reduce_rows",
    )(own, *got)


def delta_kernel(ids, s_mine, s_theirs, per_row, after, out):
    total = s_mine[...].astype(F32) + s_theirs[...].astype(F32)
    gate, up, back = total[:, 0:T], total[:, T : 2 * T], total[:, 2 * T : 3 * T]
    weight = per_row[pl.ds(pl.multiple_of(ids[2] * RB, RB), RB), :][:, 0:1]
    s = jax.nn.sigmoid(gate)
    act = gate * s
    hidden_full = act * up
    delta = back * weight
    out[0:RB, 0:T] = (delta * up * s * (1.0 + gate * (1.0 - s))).astype(BF)
    out[0:RB, T : 2 * T] = (delta * act).astype(BF)
    out[0:RB, 2 * T : 3 * T] = hidden_full.astype(BF)
    router = lax.dot_general(
        jnp.ones((8, T), F32),
        back * hidden_full,
        NT,
        precision=lax.Precision.HIGHEST,
        preferred_element_type=F32,
    )
    router = jnp.concatenate([router, jnp.zeros((8, 2 * T - RB), F32)], axis=1)
    hi, mid, low = (piece.astype(F32) for piece in split3(router))
    row = lax.broadcasted_iota(jnp.int32, (8, 2 * T), 0)
    pieces = jnp.where(row == 0, hi, jnp.where(row == 1, mid, jnp.where(row == 2, low, 0.0)))
    out[RB:MSG, 0 : 2 * T] = jnp.concatenate([pieces, jnp.zeros_like(pieces)], axis=0).astype(BF)
    out[RB:MSG, 2 * T : 3 * T] = jnp.zeros((16, T), BF)


def deltas(ids, s_mine, s_theirs, per_row, after):
    return pl.pallas_call(
        delta_kernel,
        out_shape=jax.ShapeDtypeStruct((MSG, 3 * T), BF),
        in_specs=[SMEM] + [VMEM] * 3 + [ANY],
        out_specs=VMEM,
        compiler_params=params(8),
        cost_estimate=work(20_000_000_000, 2),
        name="deltas",
    )(ids, s_mine, s_theirs, per_row, after)


def weight_grad_kernel(
    ids, tokens, out_grad, per_row, d0, d1, d2, d3, w1, w2a, w2b, w3, keep, send, flat, turned
):
    step = pl.program_id(0)
    core, x = ids[1], ids[2]

    @pl.when(step == 0)
    def _():
        for r, ref in enumerate((d0, d1, d2, d3)):
            rows = pl.ds(pl.multiple_of((x ^ r) * RB, RB), RB)
            flat[rows, :] = ref[0:RB, :]
        turned[...] = flat[...].astype(F32).T.astype(BF)

    scaled = (out_grad[...].astype(F32) * per_row[:, 0:1]).astype(BF)
    gate_up = jnp.dot(turned[0 : 2 * T, :], tokens[...], preferred_element_type=F32)
    down = jnp.dot(turned[2 * T : 3 * T, :], scaled, preferred_element_type=F32)
    for rows, value in ((slice(0, 2 * T), gate_up), (slice(2 * T, 3 * T), down)):
        low, high = value[:, 0:T].astype(BF), value[:, T : 2 * T].astype(BF)
        keep[rows, :] = jnp.where(core == 0, low, high)
        send[rows, :] = jnp.where(core == 0, high, low)


def weight_grads(ids, tokens, out_grad, per_row, parts, after):
    whole = lambda *shape: pl.BlockSpec(shape, lambda i, ids: (0,) * len(shape))
    columns = pl.BlockSpec((CAP, 2 * T), lambda i, ids: (0, ids[0] ^ far_first(i ^ 4)))
    block = pl.BlockSpec((3 * T, T), lambda i, ids: (i, 0))
    return pl.pallas_call(
        weight_grad_kernel,
        grid_spec=pltpu.PrefetchScalarGridSpec(
            num_scalar_prefetch=1,
            grid=(Z,),
            in_specs=[columns, columns, whole(CAP, T)] + [whole(MSG, 3 * T)] * 4 + [ANY] * 4,
            out_specs=[block, block],
            scratch_shapes=[pltpu.VMEM((CAP, 3 * T), BF), pltpu.VMEM((3 * T, CAP), BF)],
        ),
        out_shape=[
            jax.ShapeDtypeStruct((Z * 3 * T, T), BF),
            jax.ShapeDtypeStruct((Z * 3 * T, T), BF),
        ],
        compiler_params=params(),
        cost_estimate=work(2 * CAP * D * 3 * T, 10),
        name="weight_grads",
    )(ids, tokens, out_grad, per_row, *parts, *in_hbm(*after))


def rows_kernel(ids, d0, d1, d2, d3, after, out):
    x = ids[2]
    for r, ref in enumerate((d0, d1, d2, d3)):
        rows = pl.ds(pl.multiple_of((x ^ r) * RB, RB), RB)
        out[rows, :] = ref[0:RB, 0 : 2 * T]
        out[CAP + 16 * r : CAP + 16 * (r + 1), :] = ref[RB:MSG, 0 : 2 * T]


def row_order(ids, parts, after):
    return pl.pallas_call(
        rows_kernel,
        out_shape=jax.ShapeDtypeStruct((CAP + XS * 16, 2 * T), BF),
        in_specs=[SMEM] + [VMEM] * 4 + [ANY],
        out_specs=VMEM,
        compiler_params=params(8),
        name="row_order",
    )(ids, *parts, after)


def core_sum_kernel(keep, received, send):
    rows = slice(0, 4 * 3 * T)
    send[rows, :] = (keep[rows, :].astype(F32) + received[rows, :].astype(F32)).astype(BF)
    send[4 * 3 * T :, :] = jnp.zeros((PAD, T), BF)


def core_sum(keep, received):
    return pl.pallas_call(
        core_sum_kernel,
        out_shape=jax.ShapeDtypeStruct((4 * 3 * T + PAD, T), BF),
        in_specs=[VMEM] * 2,
        out_specs=VMEM,
        compiler_params=params(8),
        name="core_sum",
    )(keep, received)


def pair_sum_kernel(keep, received, arrived, own, s4, s2, s6):
    for i, out in enumerate((own, s4, s2, s6)):
        there = slice(i * 3 * T, (i + 1) * 3 * T)
        here = slice((i + 4) * 3 * T, (i + 5) * 3 * T)
        total = keep[here, :].astype(F32) + received[here, :].astype(F32)
        out[...] = (total + arrived[there, :].astype(F32)).astype(out.dtype)


def pair_sum(keep, received, arrived):
    part = jax.ShapeDtypeStruct((3 * T, T), BF)
    return pl.pallas_call(
        pair_sum_kernel,
        out_shape=[jax.ShapeDtypeStruct((3 * T, T), F32), part, part, part],
        in_specs=[VMEM] * 3,
        out_specs=[VMEM] * 4,
        compiler_params=params(8),
        name="pair_sum",
    )(keep, received, arrived)


def last_sum_kernel(own, r4, r2, r6, after, gate, up, down):
    total = own[...] + r4[...].astype(F32) + r2[...].astype(F32) + r6[...].astype(F32)
    gate[...] = total[0:T].T
    up[...] = total[T : 2 * T].T
    down[...] = total[2 * T : 3 * T]


def last_sum(own, r4, r2, r6, after):
    return pl.pallas_call(
        last_sum_kernel,
        out_shape=[jax.ShapeDtypeStruct((T, T), F32)] * 3,
        in_specs=[VMEM] * 4 + [ANY],
        out_specs=[VMEM] * 3,
        compiler_params=params(8),
        name="last_sum",
    )(own, r4, r2, r6, *in_hbm(after))


def token_grad_kernel(
    ids, w0, w1, w2a, w2b, w3, y0, y1, y2, y3, per_row, after, out, logits_out, router, flat
):
    step = pl.program_id(0)
    x = ids[2]
    rows_by_y = (y0, y1, y2, y3)

    @pl.when(step == 0)
    def _():
        for j in range(ROWS):
            flat[:, j * 2 * T : (j + 1) * 2 * T] = rows_by_y[j][0:CAP, :]
        for r in range(XS):
            place = pl.ds(pl.multiple_of((x ^ r) * RB, RB), RB)
            terms = []
            for j in range(ROWS):
                pieces = rows_by_y[j][CAP + 16 * r : CAP + 16 * (r + 1), :].astype(F32)
                terms.append(pieces[0:1] + pieces[1:2] + pieces[2:3])
            total = (terms[0] + terms[1]) + (terms[2] + terms[3])
            router[place, :] = turn(total)[0:RB]
        value = router[...] * per_row[:, 1:2]
        at = per_row[:, 2:3].astype(jnp.int32)
        lanes = lax.broadcasted_iota(jnp.int32, (CAP, T), 1)
        upper = jnp.where(lanes == (at >> 7), 1.0, 0.0).T.astype(BF)
        spread = jnp.where(lanes == (at & (T - 1)), value, 0.0)
        total = jnp.zeros((T, T), F32)
        for piece in split3(spread):
            total = total + jnp.dot(upper, piece, preferred_element_type=F32)
        logits_out[...] = total[0 : SEQ // T, :]

    total = jnp.zeros((CAP, WIDE), F32)
    w2 = jnp.where(step < D // WIDE // 2, w2a[...], w2b[...])
    for j, w in enumerate((w0[...], w1[...], w2, w3[...])):
        total += lax.dot_general(
            flat[:, j * 2 * T : (j + 1) * 2 * T], w, NT, preferred_element_type=F32
        )
    out[...] = total.astype(BF)


def token_grads(ids, weights, rows_by_y, per_row, after):
    whole = lambda *shape: pl.BlockSpec(shape, lambda i, ids: (0,) * len(shape))
    half = D // WIDE // 2
    tiles = lambda index: pl.BlockSpec((WIDE, 2 * T), lambda i, ids: (index(i), 0))
    return pl.pallas_call(
        token_grad_kernel,
        grid_spec=pltpu.PrefetchScalarGridSpec(
            num_scalar_prefetch=1,
            grid=(D // WIDE,),
            in_specs=[
                tiles(lambda i: i),
                tiles(lambda i: i),
                tiles(lambda i: jnp.minimum(i, half - 1)),
                tiles(lambda i: jnp.maximum(i - half, 0)),
                tiles(lambda i: i),
            ]
            + [whole(CAP + XS * 16, 2 * T)] * 4
            + [whole(CAP, T), ANY],
            out_specs=[
                pl.BlockSpec((CAP, WIDE), lambda i, ids: (0, i)),
                whole(SEQ // T, T),
            ],
            scratch_shapes=[
                pltpu.VMEM((CAP, 1), F32),
                pltpu.VMEM((CAP, 8 * T), BF),
            ],
        ),
        out_shape=[
            jax.ShapeDtypeStruct((CAP, D), BF),
            jax.ShapeDtypeStruct((SEQ // T, T), F32),
        ],
        compiler_params=params(),
        cost_estimate=work(2 * CAP * D * 8 * T, 12),
        name="token_grads",
    )(ids, *in_hbm(*weights), *rows_by_y, per_row, after)


def local(
    tokens,
    out_grad,
    router_logits,
    routed_counts,
    routed_positions,
    gate_values,
    up_values,
    down_values,
    gate_scales,
    up_scales,
    down_scales,
):
    ids = jnp.stack([lax.axis_index(axis) for axis in ("z", "core", "x")]).astype(jnp.int32)

    scales = (gate_scales.T, up_scales.T, down_scales)
    held = own_tiles(ids, *scales, gate_values, up_values, down_values)
    tokens, out_grad_early = load(tokens, out_grad)
    held = join([held] + [swap(held, "z", Z, mask) for mask in (4, 2, 6)], tokens, out_grad_early)
    mine = (held, swap(held, "z", Z, 1))
    theirs = tuple(swap(h, "core", CORES, 1) for h in mine)
    per_row = rates(router_logits.reshape(SEQ // T, T), routed_positions[None, :], routed_counts)

    own, p1, p2, p3, w_own = forward(ids, tokens, out_grad_early, mine, theirs)
    got = [swap(p, "x", XS, r) for r, p in ((1, p1), (2, p2), (3, p3))]
    total = reduce_rows(own, got)
    (out_grad,) = load(out_grad)
    message = deltas(ids, total, swap(total, "zhi", Z_HI, 1), per_row, out_grad)
    parts = [message] + [swap(message, "x", XS, r) for r in (1, 2, 3)]

    w1, w3 = (swap(w_own, "row", ROWS, r) for r in (1, 3))
    w2 = (swap(w3[: D // 2], "row", ROWS, 1), swap(w1[D // 2 :], "row", ROWS, 3))
    weights = (w_own, w1, *w2, w3)

    keep, send = weight_grads(ids, tokens, out_grad, per_row, parts, weights[1:])
    received = swap(send, "core", CORES, 1)
    sent = core_sum(keep, received)
    arrived = swap(sent, "z", Z, 1)

    rows = row_order(ids, parts, sent)
    y1, y2, y3 = (swap(rows, "row", ROWS, r) for r in (1, 2, 3))
    own_sum, s4, s2, s6 = pair_sum(keep, received, arrived)
    grad_tokens, grad_logits = token_grads(
        ids, weights, (rows, y1, y2, y3), per_row, s4
    )
    grad_gate, grad_up, grad_down = last_sum(
        own_sum,
        swap(s4, "z", Z, 4),
        swap(s2, "z", Z, 2),
        swap(s6, "z", Z, 6),
        grad_logits,
    )
    return (grad_tokens, grad_gate, grad_up, grad_down, grad_logits.reshape(SEQ))


def solution(mesh):
    fine = Mesh(mesh.devices.reshape(Z, CORES, ROWS, Z_HI, XS), AXES)
    dp, col = ("z", "core"), ("zhi", "x")
    placed = (
        P(dp, col),
        P(dp, col),
        P(dp),
        P(dp),
        P(dp),
        P(col + dp, "row"),
        P(col + dp, "row"),
        P("row", col + dp),
        P(col, "row"),
        P(col, "row"),
        P("row", col),
    )
    return jax.shard_map(
        local,
        mesh=fine,
        in_specs=placed,
        out_specs=(P(dp, col), P(col + dp, "row"), P(col + dp, "row"), P("row", col + dp), P(dp)),
        check_vma=False,
    )
```

```python
import jax
import jax.numpy as jnp
from jax import lax
from jax.experimental import pallas as pl
from jax.experimental.pallas import tpu as pltpu
from jax.sharding import Mesh, PartitionSpec as P

BF = jnp.bfloat16
F32 = jnp.float32
Z, CORES, ROWS, Z_HI, XS = 8, 2, 4, 2, 4
T = 128
CAP = 768
SEQ = 6144
D = 2048
RB = CAP // XS
PAD = 192
WIDE = 512
MSG = RB + 16
AXES = ("z", "core", "row", "zhi", "x")
NT = (((1,), (1,)), ((), ()))


def swap(value, axis, size, mask):
    return lax.ppermute(value, axis, [(i, i ^ mask) for i in range(size)])


def far_first(i):
    return ((i & 1) << 2) | (i & 2) | ((i >> 2) & 1)


def split3(value):
    hi = value.astype(BF)
    rest = value - hi.astype(F32)
    mid = rest.astype(BF)
    return hi, mid, (rest - mid.astype(F32)).astype(BF)


def params(mib=20):
    return pltpu.CompilerParams(vmem_limit_bytes=mib * 1024 * 1024)


def work(flops, mib):
    return pl.CostEstimate(flops=flops, bytes_accessed=mib * 1024 * 1024, transcendentals=0)


VMEM = pl.BlockSpec(memory_space=pltpu.VMEM)
SMEM = pl.BlockSpec(memory_space=pltpu.SMEM)
ANY = pl.BlockSpec(memory_space=pl.ANY)
HBM = pl.BlockSpec(memory_space=pltpu.HBM)


def in_hbm(*arrays):
    return tuple(pltpu.with_memory_space_constraint(array, pltpu.HBM) for array in arrays)


def turn(row):
    return jnp.broadcast_to(row, (8, row.shape[1])).T[:, 0:1]


def rates_kernel(logits, positions, counts, out):
    place = turn(positions[...].astype(F32))
    at = place.astype(jnp.int32)
    lanes = lax.broadcasted_iota(jnp.int32, (CAP, T), 1)
    upper = jnp.where(lanes[:, 0 : SEQ // T] == (at >> 7), 1.0, 0.0).astype(BF)
    picked = jnp.zeros((CAP, T), F32)
    for piece in split3(logits[...]):
        picked = picked + jnp.dot(upper, piece, preferred_element_type=F32)
    logit = jnp.sum(jnp.where(lanes == (at & (T - 1)), picked, 0.0), axis=1, keepdims=True)
    rate = jax.nn.sigmoid(logit)
    row = lax.broadcasted_iota(jnp.int32, (CAP, 1), 0)
    live = jnp.where(row < counts[0], 1.0, 0.0)
    weight = rate * live
    slope = rate * (1.0 - rate) * live
    out[...] = jnp.where(lanes == 0, weight, jnp.where(lanes == 1, slope, place))


def rates(logits, positions, counts):
    return pl.pallas_call(
        rates_kernel,
        out_shape=jax.ShapeDtypeStruct((CAP, T), F32),
        in_specs=[VMEM, VMEM, SMEM],
        out_specs=VMEM,
        compiler_params=params(8),
        name="rates",
    )(logits, positions, counts)


def tile_kernel(ids, gs, us, ds, gate, up, down, out):
    dp = ids[0] * CORES + ids[1]
    lane = lax.broadcasted_iota(jnp.int32, (1, Z * CORES), 1)
    g, u, d = (
        jnp.sum(jnp.where(lane == dp, ref[...], 0.0), axis=1, keepdims=True) for ref in (gs, us, ds)
    )
    out[:, 0:T] = (gate[...].astype(F32) * g).astype(BF)
    out[:, T : 2 * T] = (up[...].astype(F32) * u).astype(BF)
    out[:, 2 * T : 3 * T] = (down[...].astype(F32) * d).T.astype(BF)


def own_tiles(ids, gate_scales, up_scales, down_scales, gate, up, down):
    return pl.pallas_call(
        tile_kernel,
        out_shape=jax.ShapeDtypeStruct((T, 3 * T), BF),
        in_specs=[SMEM] + [VMEM] * 6,
        out_specs=VMEM,
        compiler_params=params(8),
        name="own_tiles",
    )(ids, *in_hbm(gate_scales, up_scales, down_scales, gate, up, down))


def load_kernel(*refs):
    n = len(refs) // 2
    copies = [pltpu.make_async_copy(refs[i], refs[n + i], refs[-1].at[i]) for i in range(n)]
    for copy in copies:
        copy.start()
    for copy in copies:
        copy.wait()


def load(*arrays):
    n = len(arrays)
    return pl.pallas_call(
        load_kernel,
        out_shape=[pltpu.VMEM(array.shape, array.dtype) for array in arrays],
        in_specs=[ANY] * n,
        out_specs=[ANY] * n,
        scratch_shapes=[pltpu.SemaphoreType.DMA((n,))],
        compiler_params=params(1),
        name="load",
    )(*in_hbm(*arrays))


def join_kernel(a, b, c, d, tokens, out_grad, out):
    for i, ref in enumerate((a, b, c, d)):
        out[i * T : (i + 1) * T, :] = ref[...]


def join(blocks, tokens, out_grad):
    return pl.pallas_call(
        join_kernel,
        out_shape=jax.ShapeDtypeStruct((4 * T, 3 * T), BF),
        in_specs=[VMEM] * 4 + [ANY] * 2,
        out_specs=VMEM,
        compiler_params=params(8),
        name="join",
    )(*blocks, tokens, out_grad)


def forward_kernel(ids, tokens, out_grad, m0, m1, t0, t1, own, p1, p2, p3, w_out, w_both, w_down, sem):
    step = pl.program_id(0)
    z, core = ids[0], ids[1]

    @pl.when(step == 0)
    def _():
        for i in range(Z):
            base = (z ^ far_first(i)) * (2 * T)
            for pair, side in (((m0, m1), core), ((t0, t1), 1 - core)):
                ref, j = pair[i // 4], i % 4
                rows = pl.ds(pl.multiple_of(base + side * T, T), T)
                w_both[rows, :] = ref[j * T : (j + 1) * T, 0 : 2 * T]
                w_down[rows, :] = ref[j * T : (j + 1) * T, 2 * T : 3 * T]

        pltpu.make_async_copy(w_both, w_out, sem).start()

    gate_up = jnp.dot(tokens[...], w_both[...], preferred_element_type=F32)
    back = jnp.dot(out_grad[...], w_down[...], preferred_element_type=F32)

    @pl.when(step == 0)
    def _():
        own[:, 0 : 2 * T] = gate_up
        own[:, 2 * T : 3 * T] = back

    for k, ref in ((1, p1), (2, p2), (3, p3)):

        @pl.when(step == k)
        def _():
            ref[:, 0 : 2 * T] = gate_up.astype(BF)
            ref[:, 2 * T : 3 * T] = back.astype(BF)

    @pl.when(step == XS - 1)
    def _():
        pltpu.make_async_copy(w_both, w_out, sem).wait()


def forward(ids, tokens, out_grad, mine, theirs):
    whole = lambda *shape: pl.BlockSpec(shape, lambda r, ids: (0,) * len(shape))
    rows = pl.BlockSpec((RB, D), lambda r, ids: (ids[2] ^ r, 0))
    part = pltpu.HBM((RB, 3 * T), BF)
    return pl.pallas_call(
        forward_kernel,
        grid_spec=pltpu.PrefetchScalarGridSpec(
            num_scalar_prefetch=1,
            grid=(XS,),
            in_specs=[rows, rows] + [whole(4 * T, 3 * T)] * 4,
            out_specs=[whole(RB, 3 * T)] * 4 + [ANY],
            scratch_shapes=[
                pltpu.VMEM((D, 2 * T), BF),
                pltpu.VMEM((D, T), BF),
                pltpu.SemaphoreType.DMA,
            ],
        ),
        out_shape=[
            jax.ShapeDtypeStruct((RB, 3 * T), F32),
            part,
            part,
            part,
            pltpu.HBM((D, 2 * T), BF),
        ],
        compiler_params=params(),
        cost_estimate=work(2 * CAP * D * 3 * T, 10),
        name="forward",
    )(ids, tokens, out_grad, *mine, *theirs)


def reduce_kernel(own, g1, g2, g3, total):
    total[...] = (
        own[...] + g1[...].astype(F32) + g2[...].astype(F32) + g3[...].astype(F32)
    ).astype(BF)


def reduce_rows(own, got):
    return pl.pallas_call(
        reduce_kernel,
        out_shape=jax.ShapeDtypeStruct((RB, 3 * T), BF),
        in_specs=[VMEM] * 4,
        out_specs=VMEM,
        compiler_params=params(8),
        cost_estimate=work(20_000_000_000, 2),
        name="reduce_rows",
    )(own, *got)


def delta_kernel(ids, s_mine, s_theirs, per_row, after, out):
    total = s_mine[...].astype(F32) + s_theirs[...].astype(F32)
    gate, up, back = total[:, 0:T], total[:, T : 2 * T], total[:, 2 * T : 3 * T]
    weight = per_row[pl.ds(pl.multiple_of(ids[2] * RB, RB), RB), :][:, 0:1]
    s = jax.nn.sigmoid(gate)
    act = gate * s
    hidden_full = act * up
    delta = back * weight
    out[0:RB, 0:T] = (delta * up * s * (1.0 + gate * (1.0 - s))).astype(BF)
    out[0:RB, T : 2 * T] = (delta * act).astype(BF)
    out[0:RB, 2 * T : 3 * T] = hidden_full.astype(BF)
    router = lax.dot_general(
        jnp.ones((8, T), F32),
        back * hidden_full,
        NT,
        precision=lax.Precision.HIGHEST,
        preferred_element_type=F32,
    )
    router = jnp.concatenate([router, jnp.zeros((8, 2 * T - RB), F32)], axis=1)
    hi, mid, low = (piece.astype(F32) for piece in split3(router))
    row = lax.broadcasted_iota(jnp.int32, (8, 2 * T), 0)
    pieces = jnp.where(row == 0, hi, jnp.where(row == 1, mid, jnp.where(row == 2, low, 0.0)))
    out[RB:MSG, 0 : 2 * T] = jnp.concatenate([pieces, jnp.zeros_like(pieces)], axis=0).astype(BF)
    out[RB:MSG, 2 * T : 3 * T] = jnp.zeros((16, T), BF)


def deltas(ids, s_mine, s_theirs, per_row, after):
    return pl.pallas_call(
        delta_kernel,
        out_shape=jax.ShapeDtypeStruct((MSG, 3 * T), BF),
        in_specs=[SMEM] + [VMEM] * 3 + [ANY],
        out_specs=VMEM,
        compiler_params=params(8),
        cost_estimate=work(20_000_000_000, 2),
        name="deltas",
    )(ids, s_mine, s_theirs, per_row, after)


def weight_grad_kernel(
    ids, tokens, out_grad, per_row, d0, d1, d2, d3, w1, w2a, w2b, w3, keep, send, flat, turned
):
    step = pl.program_id(0)
    core, x = ids[1], ids[2]

    @pl.when(step == 0)
    def _():
        for r, ref in enumerate((d0, d1, d2, d3)):
            rows = pl.ds(pl.multiple_of((x ^ r) * RB, RB), RB)
            flat[rows, :] = ref[0:RB, :]
        turned[...] = flat[...].astype(F32).T.astype(BF)

    scaled = (out_grad[...].astype(F32) * per_row[:, 0:1]).astype(BF)
    gate_up = jnp.dot(turned[0 : 2 * T, :], tokens[...], preferred_element_type=F32)
    down = jnp.dot(turned[2 * T : 3 * T, :], scaled, preferred_element_type=F32)
    for rows, value in ((slice(0, 2 * T), gate_up), (slice(2 * T, 3 * T), down)):
        low, high = value[:, 0:T].astype(BF), value[:, T : 2 * T].astype(BF)
        keep[rows, :] = jnp.where(core == 0, low, high)
        send[rows, :] = jnp.where(core == 0, high, low)


def weight_grads(ids, tokens, out_grad, per_row, parts, after):
    whole = lambda *shape: pl.BlockSpec(shape, lambda i, ids: (0,) * len(shape))
    columns = pl.BlockSpec((CAP, 2 * T), lambda i, ids: (0, ids[0] ^ far_first(i ^ 4)))
    block = pl.BlockSpec((3 * T, T), lambda i, ids: (i, 0))
    return pl.pallas_call(
        weight_grad_kernel,
        grid_spec=pltpu.PrefetchScalarGridSpec(
            num_scalar_prefetch=1,
            grid=(Z,),
            in_specs=[columns, columns, whole(CAP, T)] + [whole(MSG, 3 * T)] * 4 + [ANY] * 4,
            out_specs=[block, block],
            scratch_shapes=[pltpu.VMEM((CAP, 3 * T), BF), pltpu.VMEM((3 * T, CAP), BF)],
        ),
        out_shape=[
            jax.ShapeDtypeStruct((Z * 3 * T, T), BF),
            jax.ShapeDtypeStruct((Z * 3 * T, T), BF),
        ],
        compiler_params=params(),
        cost_estimate=work(2 * CAP * D * 3 * T, 10),
        name="weight_grads",
    )(ids, tokens, out_grad, per_row, *parts, *after)


def rows_kernel(ids, d0, d1, d2, d3, after, out):
    x = ids[2]
    for r, ref in enumerate((d0, d1, d2, d3)):
        rows = pl.ds(pl.multiple_of((x ^ r) * RB, RB), RB)
        out[rows, :] = ref[0:RB, 0 : 2 * T]
        out[CAP + 16 * r : CAP + 16 * (r + 1), :] = ref[RB:MSG, 0 : 2 * T]


def row_order(ids, parts, after):
    return pl.pallas_call(
        rows_kernel,
        out_shape=jax.ShapeDtypeStruct((CAP + XS * 16, 2 * T), BF),
        in_specs=[SMEM] + [VMEM] * 4 + [ANY],
        out_specs=VMEM,
        compiler_params=params(8),
        name="row_order",
    )(ids, *parts, after)


def core_sum_kernel(keep, received, send):
    rows = slice(0, 4 * 3 * T)
    send[rows, :] = (keep[rows, :].astype(F32) + received[rows, :].astype(F32)).astype(BF)
    send[4 * 3 * T :, :] = jnp.zeros((PAD, T), BF)


def core_sum(keep, received):
    return pl.pallas_call(
        core_sum_kernel,
        out_shape=jax.ShapeDtypeStruct((4 * 3 * T + PAD, T), BF),
        in_specs=[VMEM] * 2,
        out_specs=VMEM,
        compiler_params=params(8),
        name="core_sum",
    )(keep, received)


def pair_sum_kernel(keep, received, arrived, own, s4, s2, s6):
    for i, out in enumerate((own, s4, s2, s6)):
        there = slice(i * 3 * T, (i + 1) * 3 * T)
        here = slice((i + 4) * 3 * T, (i + 5) * 3 * T)
        total = keep[here, :].astype(F32) + received[here, :].astype(F32)
        out[...] = (total + arrived[there, :].astype(F32)).astype(out.dtype)


def pair_sum(keep, received, arrived):
    part = jax.ShapeDtypeStruct((3 * T, T), BF)
    return pl.pallas_call(
        pair_sum_kernel,
        out_shape=[jax.ShapeDtypeStruct((3 * T, T), F32), part, part, part],
        in_specs=[VMEM] * 3,
        out_specs=[VMEM] * 4,
        compiler_params=params(8),
        name="pair_sum",
    )(keep, received, arrived)


def last_sum_kernel(own, r4, r2, r6, after, gate, up, down):
    total = own[...] + r4[...].astype(F32) + r2[...].astype(F32) + r6[...].astype(F32)
    gate[...] = total[0:T].T
    up[...] = total[T : 2 * T].T
    down[...] = total[2 * T : 3 * T]


def last_sum(own, r4, r2, r6, after):
    return pl.pallas_call(
        last_sum_kernel,
        out_shape=[jax.ShapeDtypeStruct((T, T), F32)] * 3,
        in_specs=[VMEM] * 4 + [ANY],
        out_specs=[VMEM] * 3,
        compiler_params=params(8),
        name="last_sum",
    )(own, r4, r2, r6, *in_hbm(after))


def token_grad_kernel(
    ids, w0, w1, w2a, w2b, w3, y0, y1, y2, y3, per_row, after, out, logits_out, router, flat
):
    step = pl.program_id(0)
    x = ids[2]
    rows_by_y = (y0, y1, y2, y3)

    @pl.when(step == 0)
    def _():
        for j in range(ROWS):
            flat[:, j * 2 * T : (j + 1) * 2 * T] = rows_by_y[j][0:CAP, :]
        for r in range(XS):
            place = pl.ds(pl.multiple_of((x ^ r) * RB, RB), RB)
            terms = []
            for j in range(ROWS):
                pieces = rows_by_y[j][CAP + 16 * r : CAP + 16 * (r + 1), :].astype(F32)
                terms.append(pieces[0:1] + pieces[1:2] + pieces[2:3])
            total = (terms[0] + terms[1]) + (terms[2] + terms[3])
            router[place, :] = turn(total)[0:RB]
        value = router[...] * per_row[:, 1:2]
        at = per_row[:, 2:3].astype(jnp.int32)
        lanes = lax.broadcasted_iota(jnp.int32, (CAP, T), 1)
        upper = jnp.where(lanes == (at >> 7), 1.0, 0.0).T.astype(BF)
        spread = jnp.where(lanes == (at & (T - 1)), value, 0.0)
        total = jnp.zeros((T, T), F32)
        for piece in split3(spread):
            total = total + jnp.dot(upper, piece, preferred_element_type=F32)
        logits_out[...] = total[0 : SEQ // T, :]

    total = jnp.zeros((CAP, WIDE), F32)
    w2 = jnp.where(step < D // WIDE // 2, w2a[...], w2b[...])
    for j, w in enumerate((w0[...], w1[...], w2, w3[...])):
        total += lax.dot_general(
            flat[:, j * 2 * T : (j + 1) * 2 * T], w, NT, preferred_element_type=F32
        )
    out[...] = total.astype(BF)


def token_grads(ids, weights, rows_by_y, per_row, after):
    whole = lambda *shape: pl.BlockSpec(shape, lambda i, ids: (0,) * len(shape))
    half = D // WIDE // 2
    tiles = lambda index: pl.BlockSpec((WIDE, 2 * T), lambda i, ids: (index(i), 0))
    return pl.pallas_call(
        token_grad_kernel,
        grid_spec=pltpu.PrefetchScalarGridSpec(
            num_scalar_prefetch=1,
            grid=(D // WIDE,),
            in_specs=[
                tiles(lambda i: i),
                tiles(lambda i: i),
                tiles(lambda i: jnp.minimum(i, half - 1)),
                tiles(lambda i: jnp.maximum(i - half, 0)),
                tiles(lambda i: i),
            ]
            + [whole(CAP + XS * 16, 2 * T)] * 4
            + [whole(CAP, T), ANY],
            out_specs=[
                pl.BlockSpec((CAP, WIDE), lambda i, ids: (0, i)),
                whole(SEQ // T, T),
            ],
            scratch_shapes=[
                pltpu.VMEM((CAP, 1), F32),
                pltpu.VMEM((CAP, 8 * T), BF),
            ],
        ),
        out_shape=[
            jax.ShapeDtypeStruct((CAP, D), BF),
            jax.ShapeDtypeStruct((SEQ // T, T), F32),
        ],
        compiler_params=params(),
        cost_estimate=work(2 * CAP * D * 8 * T, 12),
        name="token_grads",
    )(ids, *in_hbm(*weights), *rows_by_y, per_row, after)


def local(
    tokens,
    out_grad,
    router_logits,
    routed_counts,
    routed_positions,
    gate_values,
    up_values,
    down_values,
    gate_scales,
    up_scales,
    down_scales,
):
    ids = jnp.stack([lax.axis_index(axis) for axis in ("z", "core", "x")]).astype(jnp.int32)

    scales = (gate_scales.T, up_scales.T, down_scales)
    held = own_tiles(ids, *scales, gate_values, up_values, down_values)
    tokens, out_grad_early = load(tokens, out_grad)
    held = join([held] + [swap(held, "z", Z, mask) for mask in (4, 2, 6)], tokens, out_grad_early)
    mine = (held, swap(held, "z", Z, 1))
    theirs = tuple(swap(h, "core", CORES, 1) for h in mine)
    per_row = rates(router_logits.reshape(SEQ // T, T), routed_positions[None, :], routed_counts)

    own, p1, p2, p3, w_own = forward(ids, tokens, out_grad_early, mine, theirs)
    got = [swap(p, "x", XS, r) for r, p in ((1, p1), (2, p2), (3, p3))]
    total = reduce_rows(own, got)
    (out_grad,) = load(out_grad)
    message = deltas(ids, total, swap(total, "zhi", Z_HI, 1), per_row, out_grad)
    parts = [message] + [swap(message, "x", XS, r) for r in (1, 2, 3)]

    w1, w3 = (swap(w_own, "row", ROWS, r) for r in (1, 3))
    w2 = (swap(w3[: D // 2], "row", ROWS, 1), swap(w1[D // 2 :], "row", ROWS, 3))
    weights = (w_own, w1, *w2, w3)

    keep, send = weight_grads(ids, tokens, out_grad, per_row, parts, weights[1:])
    received = swap(send, "core", CORES, 1)
    sent = core_sum(keep, received)
    arrived = swap(sent, "z", Z, 1)

    rows = row_order(ids, parts, sent)
    y1, y2, y3 = (swap(rows, "row", ROWS, r) for r in (1, 2, 3))
    own_sum, s4, s2, s6 = pair_sum(keep, received, arrived)
    grad_tokens, grad_logits = token_grads(
        ids, weights, (rows, y1, y2, y3), per_row, s4
    )
    grad_gate, grad_up, grad_down = last_sum(
        own_sum,
        swap(s4, "z", Z, 4),
        swap(s2, "z", Z, 2),
        swap(s6, "z", Z, 6),
        grad_logits,
    )
    return (grad_tokens, grad_gate, grad_up, grad_down, grad_logits.reshape(SEQ))


def solution(mesh):
    fine = Mesh(mesh.devices.reshape(Z, CORES, ROWS, Z_HI, XS), AXES)
    dp, col = ("z", "core"), ("zhi", "x")
    placed = (
        P(dp, col),
        P(dp, col),
        P(dp),
        P(dp),
        P(dp),
        P(col + dp, "row"),
        P(col + dp, "row"),
        P("row", col + dp),
        P(col, "row"),
        P(col, "row"),
        P("row", col),
    )
    return jax.shard_map(
        local,
        mesh=fine,
        in_specs=placed,
        out_specs=(P(dp, col), P(col + dp, "row"), P(col + dp, "row"), P("row", col + dp), P(dp)),
        check_vma=False,
    )
```
